128 devices in a mesh: task: 8 (over y, z_hi), row: 2 (over core), col: 8 (over z_lo, x).
Axes of the slice: x: 4, y: 4, z: 4 (z_hi: 2, z_lo: 2; z = z_hi * 2 + z_lo), core: 2. Of those that a mesh axis runs over, the one named last changes fastest.
Arguments:
- inputs: bfloat16 [8, 512, 4096], P('task', None, 'row'), may hold values from -6 to 6
- gate_weight: bfloat16 [8, 4096, 10240], P('task', 'row', 'col'), may hold values from -0.09375 to 0.09375
- up_weight: bfloat16 [8, 4096, 10240], P('task', 'row', 'col'), may hold values from -0.09375 to 0.09375
- cotangent: bfloat16 [8, 512, 4096], P('task', None, ('row', 'col')), may hold values from -0.59765625 to 0.59765625
- down_weight: bfloat16 [8, 10240, 4096], P('task', 'col', 'row'), may hold values from -6 to 6
Outputs:
- merged: bfloat16 [10240, 4096], P('col', 'row')
The draws below stay inside these ranges and needn't reach their ends.
All inputs are finite; a program needn't handle non-finite values.
Results may differ from the reference program's by a relative error of at most 0.0095.
Values may be sent and summed in bfloat16 or wider, within the bound.
No kernel may reach another device: no remote copies, remote signals or barrier semaphores. Data moves between devices by JAX's collectives and lax.ppermute only.
A program may use at most 192 MiB of HBM per device.

```python
import jax
import jax.numpy as jnp
from jax import lax

D = 4096
FF = 10240
EX = 4
LEN = 128
TASKS = 8
TOK = 512


def level_of(stream_key, shape, pieces, least, largest):
    factor_of = 1.0
    for axis_at, blocks in pieces:
        draws = jax.random.uniform(jax.random.fold_in(jax.random.fold_in(stream_key, 6), axis_at), (blocks,), jnp.float32, least / len(pieces), largest / len(pieces))
        factor_of = factor_of * jnp.repeat(jnp.exp(draws), shape[axis_at] // blocks).reshape((-1,) + (1,) * (len(shape) - 1 - axis_at))
    return factor_of


def scatter_about(key, dims, width, most, shards=(), kind=jnp.bfloat16):
    factor_of = level_of(key, dims, shards, -0.22, 0.18) if shards else 1.0
    array = jax.random.normal(key, dims, jnp.float32) * width * factor_of
    return jnp.minimum(jnp.maximum(array, -most), most).astype(kind)


def setup_inputs(seed: int = 0) -> dict:
    key_list = jax.random.split(jax.random.key(seed), 6)
    inputs = scatter_about(key_list[0], (TASKS, TOK, D), 1.0, 6.0, ((0, 8), (2, 2)))
    gate_weight = scatter_about(key_list[1], (TASKS, D, FF), D ** -0.5, 0.09375, ((0, 8), (1, 2), (2, 8)))
    up_weight = scatter_about(key_list[2], (TASKS, D, FF), D ** -0.5, 0.09375, ((0, 8), (1, 2), (2, 8)))
    cotangent = scatter_about(key_list[3], (TASKS, TOK, D), 0.1, 0.59765625, ((0, 8), (2, 16)))
    down_weight = scatter_about(key_list[4], (TASKS, FF, D), 1.0, 6.0, ((0, 8), (1, 8), (2, 2)))
    return dict(inputs=inputs, gate_weight=gate_weight, up_weight=up_weight, cotangent=cotangent, down_weight=down_weight)


fisher_floor = 0.05


def one_task(inputs, gate_weight, up_weight, cotangent, down_weight):
    gate = jnp.dot(inputs, gate_weight, preferred_element_type=jnp.float32)
    up = jnp.dot(inputs, up_weight, preferred_element_type=jnp.float32)
    hidden = (jax.nn.gelu(gate, approximate=True) * up).astype(jnp.bfloat16)

    def accumulate(total, step):
        start = (step * LEN).astype(jnp.int32)
        h_rows = lax.dynamic_slice_in_dim(hidden, start, LEN, 0)
        d_rows = lax.dynamic_slice_in_dim(cotangent, start, LEN, 0)
        grad = lax.dot_general(h_rows, d_rows, (((0,), (0,)), ((), ())), preferred_element_type=jnp.float32)
        return total + grad * grad, None

    fisher, unused = lax.scan(accumulate, jnp.zeros((FF, D), jnp.float32), jnp.arange(EX, dtype=jnp.int32))
    weight = fisher + fisher_floor
    term = weight * down_weight.astype(jnp.float32)
    return term, weight.astype(jnp.bfloat16)


def reference(inputs, gate_weight, up_weight, cotangent, down_weight):
    def add_task(carry, index):
        term, weight = one_task(inputs[index], gate_weight[index], up_weight[index], cotangent[index], down_weight[index])
        return (carry[0] + term, carry[1] + weight.astype(jnp.float32)), None

    start = (jnp.zeros((FF, D), jnp.float32), jnp.zeros((FF, D), jnp.float32))
    totals, unused = lax.scan(add_task, start, jnp.arange(TASKS, dtype=jnp.int32))
    return (totals[0] / totals[1]).astype(jnp.bfloat16)
```

```python
import functools

import jax
import jax.numpy as jnp
from jax import lax
from jax.experimental import pallas as pl
from jax.experimental.pallas import tpu as pltpu
from jax.sharding import PartitionSpec as P

LEN = 128
HALF = 256
BLK = 256
fisher_floor = 0.05
F32 = jnp.float32
BF = jnp.bfloat16
VMEM = pl.BlockSpec(memory_space=pltpu.VMEM)
SMEM = pl.BlockSpec(memory_space=pltpu.SMEM)
ANY = pl.BlockSpec(memory_space=pl.ANY)
HBM = pl.BlockSpec(memory_space=pltpu.HBM)
TOKEN = jax.ShapeDtypeStruct((8, 128), F32)
FREE = pl.CostEstimate(flops=0, bytes_accessed=0, transcendentals=0)


def task_of(y, h):
    return y * 2 + h


def y_shift(n):
    return [(task_of(y, h), task_of((y + n) % 4, h)) for y in range(4) for h in range(2)]


def x_shift(n):
    return [(z * 4 + x, z * 4 + (x + n) % 4) for z in range(2) for x in range(4)]


Z_SWAP = [(task_of(y, h), task_of(y, 1 - h)) for y in range(4) for h in range(2)]
ZLO_SWAP = [(c, (c + 4) % 8) for c in range(8)]
CORE_SWAP = [(0, 1), (1, 0)]
X_GROUPS = [[z * 4 + x for x in range(4)] for z in range(2)]
Z_MIRROR = [
    (task_of(y, h) * 8 + c, task_of(y, 1 - h) * 8 + (c + 4) % 8) for y in range(4) for h in range(2) for c in range(8)
]
RING = [
    (task_of(y, h) * 2 + r, task_of((y + (1 if r == 0 else -1)) % 4, h) * 2 + r)
    for y in range(4)
    for h in range(2)
    for r in range(2)
]


def move(x, perm, axis="task"):
    return lax.ppermute(x, axis, perm)


def project_kernel(step, offs, x_hbm, g_hbm, u_hbm, own_ref, send_ref, token, x_ref, p_ref, sum_ref, sem):
    depth, width = g_hbm.shape
    steps = depth // step
    copies = []

    def fetch(src, dst):
        copy = pltpu.make_async_copy(src, dst, sem.at[len(copies)])
        copy.start()
        copies.append(copy)

    for half, side in enumerate((offs[0], 1 - offs[0])):
        rows = pl.ds(pl.multiple_of(side * HALF, HALF), HALF)
        fetch(x_hbm.at[rows, :], x_ref.at[pl.ds(half * HALF, HALF), :])
    for n in range(steps):
        for i, hbm in enumerate((g_hbm, u_hbm)):
            fetch(hbm.at[pl.ds(n * step, step), :], p_ref.at[i, pl.ds(n * step, step), :])
    token[...] = jnp.zeros_like(token)
    copies[0].wait()
    copies[1].wait()
    for n in range(steps):
        deep = pl.ds(n * step, step)
        for i in range(2):
            copies[2 + 2 * n + i].wait()
            for c in range(width // BLK):
                cols = pl.ds(c * BLK, BLK)
                both = jnp.dot(x_ref[:, deep], p_ref[i, deep, cols], preferred_element_type=F32)
                mine, other = both[:HALF], both[HALF:]
                if n > 0:
                    mine = mine + own_ref[i, :, cols]
                    other = other + sum_ref[i, :, cols]
                own_ref[i, :, cols] = mine
                if n < steps - 1:
                    sum_ref[i, :, cols] = other
                else:
                    send_ref[i, :, cols] = other.astype(BF)


def project(offs, x, w_gate, w_up):
    depth, width = w_gate.shape
    step = 512
    return pl.pallas_call(
        functools.partial(project_kernel, step),
        in_specs=[SMEM] + [HBM] * 3,
        out_specs=[VMEM] * 3,
        out_shape=[
            jax.ShapeDtypeStruct((2, HALF, width), F32),
            jax.ShapeDtypeStruct((2, HALF, width), BF),
            TOKEN,
        ],
        scratch_shapes=[
            pltpu.VMEM(x.shape, BF),
            pltpu.VMEM((2, depth, width), BF),
            pltpu.VMEM((2, HALF, width), F32),
            pltpu.SemaphoreType.DMA((2 + 2 * (depth // step),)),
        ],
        compiler_params=pltpu.CompilerParams(vmem_limit_bytes=22 * 2**20),
        cost_estimate=FREE,
    )(offs, in_hbm(x), in_hbm(w_gate), in_hbm(w_up))


def pass_kernel(n, *refs):
    refs[-1][...] = jnp.zeros_like(refs[-1])


def hold(x, before):
    return pl.pallas_call(
        functools.partial(pass_kernel, len(before)),
        in_specs=[VMEM] * (1 + len(before)),
        out_specs=[VMEM, VMEM],
        out_shape=[jax.ShapeDtypeStruct(x.shape, x.dtype), TOKEN],
        input_output_aliases={0: 0},
        compiler_params=pltpu.CompilerParams(vmem_limit_bytes=2**20),
        cost_estimate=FREE,
    )(x, *before)


def hidden_kernel(offs, own_ref, recv_ref, w_ref, *refs):
    out_ref, away_ref, w_away_ref, token = refs[-4:]
    token[...] = jnp.zeros_like(token)
    step = 256
    for n in range(out_ref.shape[0] // step):
        cols = pl.ds(n * step, step)
        gate = own_ref[0, :, cols] + recv_ref[0, :, cols].astype(F32)
        up = own_ref[1, :, cols] + recv_ref[1, :, cols].astype(F32)
        hidden = jax.nn.gelu(gate, approximate=True) * up
        out_ref[cols, :] = hidden.T.astype(BF)
    half, wide = w_away_ref.shape
    rows = pl.ds(pl.multiple_of(offs[1], 16), half)
    away_ref[...] = out_ref[rows, :]
    w_away_ref[...] = w_ref[rows, pl.ds(pl.multiple_of(offs[2], BLK), wide)]


def make_hidden(offs, own, recv, w, before):
    width = own.shape[2]
    return pl.pallas_call(
        hidden_kernel,
        in_specs=[SMEM, VMEM, VMEM, VMEM] + [VMEM] * len(before),
        out_specs=[VMEM] * 4,
        out_shape=[
            jax.ShapeDtypeStruct((width, HALF), BF),
            jax.ShapeDtypeStruct((width // 2, HALF), BF),
            jax.ShapeDtypeStruct((w.shape[0] // 2, w.shape[1] // 2), BF),
            TOKEN,
        ],
        compiler_params=pltpu.CompilerParams(vmem_limit_bytes=6 * 2**20),
        cost_estimate=FREE,
    )(offs, own, recv, w, *before)


def join_kernel(n, *refs):
    parts, out, token = refs[:n], refs[-2], refs[-1]
    token[...] = jnp.zeros_like(token)
    for i in range(n):
        out[i] = parts[i][...]


def join(parts, token):
    return pl.pallas_call(
        functools.partial(join_kernel, len(parts)),
        in_specs=[VMEM] * (len(parts) + 1),
        out_specs=[VMEM, VMEM],
        out_shape=[jax.ShapeDtypeStruct((len(parts), *parts[0].shape), BF), TOKEN],
        compiler_params=pltpu.CompilerParams(vmem_limit_bytes=6 * 2**20),
        cost_estimate=FREE,
    )(*parts, token)


def term_kernel(rows, nb, spots, kinds, n_recv, final, offs, *refs):
    refs = list(refs)
    parts = []
    for kind in kinds:
        ha, hb, d = refs.pop(0), refs.pop(0), [refs.pop(0) for _ in range(nb)]
        parts.append((ha, hb, d, kind, refs.pop(0)))
    recv = [refs.pop(0) for _ in range(n_recv)]
    out, token = refs[-2:]
    token[...] = jnp.zeros_like(token)
    tile = next(t for t in (160, 128, 112, 96, 80, 64, 48, 32, 16) if rows % t == 0)
    toks = (offs[0] * HALF, (1 - offs[0]) * HALF)
    for j in range(nb):
        cols = pl.ds(j * BLK, BLK)

        @pl.loop(0, rows // tile)
        def _(i):
            at = pl.multiple_of(i * tile, 16)
            here = pl.ds(at, tile)
            num = den = None
            for (ha, hb, d, kind, w), (h_spot, w_row_spot, w_col_spot) in zip(parts, spots):
                row = pl.multiple_of(offs[h_spot] + at, 16)
                w_row = pl.multiple_of(offs[w_row_spot] + at, 16)
                w_col = pl.multiple_of(offs[w_col_spot + j], BLK)
                weight = jnp.full((tile, BLK), fisher_floor, F32)
                for h, tok in zip((ha, hb), toks):
                    for e in range(2):
                        there = pl.ds(pl.multiple_of(tok + e * LEN, LEN), LEN)
                        grad = jnp.dot(
                            h[pl.ds(row, tile), e * LEN : (e + 1) * LEN],
                            d[j][there, :] if kind is None else d[j][kind, there, :],
                            preferred_element_type=F32,
                        )
                        weight = weight + grad * grad
                term = weight * w[pl.ds(w_row, tile), pl.ds(w_col, BLK)].astype(F32)
                num = term if num is None else num + term
                den = weight if den is None else den + weight
            for ref in recv:
                num = num + ref[0, here, cols].astype(F32)
                den = den + ref[1, here, cols].astype(F32)
            if final:
                out[here, cols] = (num / den).astype(BF)
            else:
                out[0, here, cols] = num.astype(BF)
                out[1, here, cols] = den.astype(BF)


def terms(offs, sources, rows, recv, final, before):
    nb = len(sources[0][2])
    wide = nb * BLK
    operands = [offs]
    for ha, hb, d, kind, w, spots in sources:
        operands += [ha, hb, *d, w]
    operands += [*recv, *before]
    return pl.pallas_call(
        functools.partial(term_kernel, rows, nb, [s[5] for s in sources], [s[3] for s in sources], len(recv), final),
        in_specs=[SMEM] + [VMEM] * (len(operands) - 1),
        out_specs=[VMEM, VMEM],
        out_shape=[jax.ShapeDtypeStruct((rows, wide) if final else (2, rows, wide), BF), TOKEN],
        compiler_params=pltpu.CompilerParams(vmem_limit_bytes=6 * 2**20),
        cost_estimate=FREE,
    )(*operands)


def merge_kernel(a, b, before, out, token):
    token[...] = jnp.zeros_like(token)
    num = a[0].astype(F32) + b[0].astype(F32)
    den = a[1].astype(F32) + b[1].astype(F32)
    out[...] = (num / den).astype(BF)


def merge(a, b, token):
    return pl.pallas_call(
        merge_kernel,
        in_specs=[VMEM] * 3,
        out_specs=[VMEM, VMEM],
        out_shape=[jax.ShapeDtypeStruct(a.shape[1:], BF), TOKEN],
        compiler_params=pltpu.CompilerParams(vmem_limit_bytes=6 * 2**20),
        cost_estimate=FREE,
    )(a, b, token)


def place_kernel(plan, n_parts, offs, *refs):
    parts, out, sem = refs[:n_parts], refs[-2], refs[-1]
    copies = []
    for part, lead, rows, row_at, col_at, nb in plan:
        src = parts[part] if lead is None else parts[part].at[lead]
        row = pl.multiple_of(offs[row_at], 16)
        for j in range(nb):
            col = pl.multiple_of(offs[col_at + j], BLK)
            copy = pltpu.make_async_copy(
                src.at[:, pl.ds(j * BLK, BLK)], out.at[pl.ds(row, rows), pl.ds(col, BLK)], sem.at[len(copies)]
            )
            copy.start()
            copies.append(copy)
    for copy in copies:
        copy.wait()


def place(shape, offs, parts, plan, before):
    return pl.pallas_call(
        functools.partial(place_kernel, plan, len(parts)),
        in_specs=[SMEM] + [VMEM] * (len(parts) + len(before)),
        out_specs=HBM,
        out_shape=jax.ShapeDtypeStruct(shape, BF),
        scratch_shapes=[pltpu.SemaphoreType.DMA((sum(p[-1] for p in plan),))],
        compiler_params=pltpu.CompilerParams(vmem_limit_bytes=2**20),
        cost_estimate=FREE,
    )(offs, *parts, *before)


def in_hbm(x):
    return pltpu.with_memory_space_constraint(x, pltpu.HBM)


def ints(*values):
    return jnp.stack([jnp.asarray(v, jnp.int32) for v in values])


def body(inputs, gate_weight, up_weight, cotangent, down_weight):
    task, core, col = lax.axis_index("task"), lax.axis_index("row"), lax.axis_index("col")
    y, h = task // 2, task % 2
    z_lo, x = col // 4, col % 4
    ring = 1 - 2 * core
    width, wide = down_weight.shape[1:]
    half, quarter, part = width // 2, width // 4, width // 8
    table = [core, (1 - h) * half, (1 - z_lo) * (wide // 2)]
    block = [(x - n) % 4 * BLK for n in range(4)]
    NEAR = len(table)
    table += [z_lo * (wide // 2) + b for b in block]
    FAR = len(table)
    table += [(1 - z_lo) * (wide // 2) + b for b in block]
    ALONE = len(table)
    table += block
    RING_ROW = len(table)
    table += [(y - k * ring) % 4 * quarter for k in range(4)]
    PART = len(table)
    table += [(y - k * ring) % 4 * part for k in range(4)]
    HERE = len(table)
    table += [h * half + (y - k * ring) % 4 * part for k in range(4)]
    BACK = len(table)
    table += [(y - k) % 4 * quarter for k in range(4)]
    BACK_HERE = len(table)
    table += [h * half + (y - k) % 4 * part for k in range(4)]
    BACK_AWAY = len(table)
    table += [(1 - h) * half + (y - k) % 4 * part for k in range(4)]
    offs = ints(*table)

    mine = cotangent[0]
    near = [mine] + [move(mine, x_shift(n), "col") for n in (1, 2, 3)]
    far_mine = [move(mine, ZLO_SWAP, "col"), move(mine, Z_MIRROR, ("task", "col"))]
    w = down_weight[0]
    own, send, token = project(offs, inputs[0], gate_weight[0], up_weight[0])
    send, token = hold(send, [token, near[1], near[3]])
    ha, away, w_there, token = make_hidden(offs, own, move(send, CORE_SWAP, "row"), w, [token])
    w_here = move(w_there, Z_SWAP)
    hb = move(ha, CORE_SWAP, "row")
    za = move(away, Z_SWAP)
    zb = move(za, CORE_SWAP, "row")

    def ring_terms(p, k, recv, *before):
        at = RING_ROW + k
        d = near[2 * p : 2 * p + 2]
        return terms(offs, [(ha, hb, d, None, w, (at, at, NEAR + 2 * p))], quarter, recv, False, before)

    def far_terms(k, recv, final, *before):
        return terms(
            offs,
            [
                (ha, hb, far, 0, w, (HERE + k, HERE + k, FAR)),
                (za, zb, far, 1, w_here, (PART + k, PART + k, ALONE)),
            ],
            part, recv, final, before,
        )

    got = [(), ()]
    for k in (1, 2, 3):
        for p in range(2):
            extra = {(3, 0): lambda: [za], (3, 1): lambda: [zb, w_here]}.get((k, p), list)()
            piece, token = ring_terms(p, k, got[p], token, *extra)
            got[p] = (move(piece, RING, ("task", "row")),)
            if (k, p) == (2, 0):
                far_pair, token = join(far_mine, token)
                far = [far_pair] + [move(far_pair, x_shift(n), "col") for n in (1, 2, 3)]
    a_sum, a_got, a_all = [None, None], [None, None], [None, None]
    a_sum[0], token = ring_terms(0, 0, got[0], token)
    a_got[0] = move(a_sum[0], Z_SWAP)
    b_got = ()
    for k in (1, 2, 3):
        piece, token = far_terms(k, b_got, False, token)
        b_got = (move(piece, RING, ("task", "row")),)
        if k == 1:
            a_sum[1], token = ring_terms(1, 0, got[1], token)
            a_got[1] = move(a_sum[1], Z_SWAP)
        if k == 2:
            out, token = merge(a_sum[0], a_got[0], token)
            a_all[0] = [out] + [move(out, y_shift(k)) for k in (1, 2, 3)]
        if k == 3:
            out, token = merge(a_sum[1], a_got[1], token)
            a_all[1] = [out] + [move(out, y_shift(k)) for k in (1, 2, 3)]
    b_out, token = far_terms(0, b_got, True, token)
    b_near = [b_out] + [move(b_out, y_shift(k)) for k in (1, 2, 3)]
    b_far = [move(piece, Z_SWAP) for piece in b_near]

    plan = []
    for k in range(4):
        plan += [(4 * p + k, None, quarter, BACK + k, NEAR + 2 * p, 2) for p in range(2)]
        plan += [(8 + k, None, part, BACK_HERE + k, FAR, 4), (12 + k, None, part, BACK_AWAY + k, FAR, 4)]
    return place((width, wide), offs, [*a_all[0], *a_all[1], *b_near, *b_far], plan, [token])


def solution(mesh):
    placed = (
        P("task", None, "row"),
        P("task", "row", "col"),
        P("task", "row", "col"),
        P("task", None, ("row", "col")),
        P("task", "col", "row"),
    )
    return jax.shard_map(
        body, mesh=mesh, in_specs=placed, out_specs=P("col", "row"), check_vma=False
    )
```

```python
import functools

import jax
import jax.numpy as jnp
from jax import lax
from jax.experimental import pallas as pl
from jax.experimental.pallas import tpu as pltpu
from jax.sharding import PartitionSpec as P

LEN = 128
HALF = 256
BLK = 256
fisher_floor = 0.05
F32 = jnp.float32
BF = jnp.bfloat16
VMEM = pl.BlockSpec(memory_space=pltpu.VMEM)
SMEM = pl.BlockSpec(memory_space=pltpu.SMEM)
ANY = pl.BlockSpec(memory_space=pl.ANY)
HBM = pl.BlockSpec(memory_space=pltpu.HBM)
TOKEN = jax.ShapeDtypeStruct((8, 128), F32)
FREE = pl.CostEstimate(flops=0, bytes_accessed=0, transcendentals=0)


def task_of(y, h):
    return y * 2 + h


def y_shift(n):
    return [(task_of(y, h), task_of((y + n) % 4, h)) for y in range(4) for h in range(2)]


def x_shift(n):
    return [(z * 4 + x, z * 4 + (x + n) % 4) for z in range(2) for x in range(4)]


Z_SWAP = [(task_of(y, h), task_of(y, 1 - h)) for y in range(4) for h in range(2)]
ZLO_SWAP = [(c, (c + 4) % 8) for c in range(8)]
CORE_SWAP = [(0, 1), (1, 0)]
X_GROUPS = [[z * 4 + x for x in range(4)] for z in range(2)]
Z_MIRROR = [
    (task_of(y, h) * 8 + c, task_of(y, 1 - h) * 8 + (c + 4) % 8) for y in range(4) for h in range(2) for c in range(8)
]
RING = [
    (task_of(y, h) * 2 + r, task_of((y + (1 if r == 0 else -1)) % 4, h) * 2 + r)
    for y in range(4)
    for h in range(2)
    for r in range(2)
]


def move(x, perm, axis="task"):
    return lax.ppermute(x, axis, perm)


def project_kernel(step, offs, x_hbm, g_hbm, u_hbm, own_ref, send_ref, token, x_ref, p_ref, sum_ref, sem):
    depth, width = g_hbm.shape
    steps = depth // step
    copies = []

    def fetch(src, dst):
        copy = pltpu.make_async_copy(src, dst, sem.at[len(copies)])
        copy.start()
        copies.append(copy)

    for half, side in enumerate((offs[0], 1 - offs[0])):
        rows = pl.ds(pl.multiple_of(side * HALF, HALF), HALF)
        fetch(x_hbm.at[rows, :], x_ref.at[pl.ds(half * HALF, HALF), :])
    for n in range(steps):
        for i, hbm in enumerate((g_hbm, u_hbm)):
            fetch(hbm.at[pl.ds(n * step, step), :], p_ref.at[i, pl.ds(n * step, step), :])
    token[...] = jnp.zeros_like(token)
    copies[0].wait()
    copies[1].wait()
    for n in range(steps):
        deep = pl.ds(n * step, step)
        for i in range(2):
            copies[2 + 2 * n + i].wait()
            for c in range(width // BLK):
                cols = pl.ds(c * BLK, BLK)
                both = jnp.dot(x_ref[:, deep], p_ref[i, deep, cols], preferred_element_type=F32)
                mine, other = both[:HALF], both[HALF:]
                if n > 0:
                    mine = mine + own_ref[i, :, cols]
                    other = other + sum_ref[i, :, cols]
                own_ref[i, :, cols] = mine
                if n < steps - 1:
                    sum_ref[i, :, cols] = other
                else:
                    send_ref[i, :, cols] = other.astype(BF)


def project(offs, x, w_gate, w_up):
    depth, width = w_gate.shape
    step = 512
    return pl.pallas_call(
        functools.partial(project_kernel, step),
        in_specs=[SMEM] + [HBM] * 3,
        out_specs=[VMEM] * 3,
        out_shape=[
            jax.ShapeDtypeStruct((2, HALF, width), F32),
            jax.ShapeDtypeStruct((2, HALF, width), BF),
            TOKEN,
        ],
        scratch_shapes=[
            pltpu.VMEM(x.shape, BF),
            pltpu.VMEM((2, depth, width), BF),
            pltpu.VMEM((2, HALF, width), F32),
            pltpu.SemaphoreType.DMA((2 + 2 * (depth // step),)),
        ],
        compiler_params=pltpu.CompilerParams(vmem_limit_bytes=22 * 2**20),
        cost_estimate=FREE,
    )(offs, in_hbm(x), in_hbm(w_gate), in_hbm(w_up))


def pass_kernel(n, *refs):
    refs[-1][...] = jnp.zeros_like(refs[-1])


def hold(x, before):
    return pl.pallas_call(
        functools.partial(pass_kernel, len(before)),
        in_specs=[VMEM] * (1 + len(before)),
        out_specs=[VMEM, VMEM],
        out_shape=[jax.ShapeDtypeStruct(x.shape, x.dtype), TOKEN],
        input_output_aliases={0: 0},
        compiler_params=pltpu.CompilerParams(vmem_limit_bytes=2**20),
        cost_estimate=FREE,
    )(x, *before)


def hidden_kernel(offs, own_ref, recv_ref, w_ref, c0_ref, c1_ref, *refs):
    out_ref, away_ref, pair_ref, token = refs[-4:]
    token[...] = jnp.zeros_like(token)
    step = 256
    for n in range(out_ref.shape[0] // step):
        cols = pl.ds(n * step, step)
        gate = own_ref[0, :, cols] + recv_ref[0, :, cols].astype(F32)
        up = own_ref[1, :, cols] + recv_ref[1, :, cols].astype(F32)
        hidden = jax.nn.gelu(gate, approximate=True) * up
        out_ref[cols, :] = hidden.T.astype(BF)
    half, wide = away_ref.shape
    wide -= HALF
    rows = pl.ds(pl.multiple_of(offs[1], 16), half)
    away_ref[:, wide:] = out_ref[rows, :]
    away_ref[:, :wide] = w_ref[rows, pl.ds(pl.multiple_of(offs[2], BLK), wide)]
    pair_ref[0] = c0_ref[...]
    pair_ref[1] = c1_ref[...]


def make_hidden(offs, own, recv, w, pair, before):
    width = own.shape[2]
    return pl.pallas_call(
        hidden_kernel,
        in_specs=[SMEM] + [VMEM] * (5 + len(before)),
        out_specs=[VMEM] * 4,
        out_shape=[
            jax.ShapeDtypeStruct((width, HALF), BF),
            jax.ShapeDtypeStruct((w.shape[0] // 2, w.shape[1] // 2 + HALF), BF),
            jax.ShapeDtypeStruct((2, *pair[0].shape), BF),
            TOKEN,
        ],
        compiler_params=pltpu.CompilerParams(vmem_limit_bytes=6 * 2**20),
        cost_estimate=FREE,
    )(offs, own, recv, w, *pair, *before)


def cut_kernel(a_ref, before, out_ref, token):
    token[...] = jnp.zeros_like(token)
    out_ref[...] = a_ref[:, a_ref.shape[1] - out_ref.shape[1] :]


def cut(a, wide, token):
    return pl.pallas_call(
        cut_kernel,
        in_specs=[VMEM, VMEM],
        out_specs=[VMEM, VMEM],
        out_shape=[jax.ShapeDtypeStruct((a.shape[0], wide), BF), TOKEN],
        compiler_params=pltpu.CompilerParams(vmem_limit_bytes=6 * 2**20),
        cost_estimate=FREE,
    )(a, token)


def term_kernel(rows, nb, spots, kinds, n_recv, final, offs, *refs):
    refs = list(refs)
    parts = []
    for kind in kinds:
        ha, hb, d = refs.pop(0), refs.pop(0), [refs.pop(0) for _ in range(nb)]
        parts.append((ha, hb, d, kind, refs.pop(0)))
    recv = [refs.pop(0) for _ in range(n_recv)]
    out, token = refs[-2:]
    token[...] = jnp.zeros_like(token)
    tile = next(t for t in (160, 128, 112, 96, 80, 64, 48, 32, 16) if rows % t == 0)
    toks = (offs[0] * HALF, (1 - offs[0]) * HALF)
    for j in range(nb):
        cols = pl.ds(j * BLK, BLK)

        @pl.loop(0, rows // tile)
        def _(i):
            at = pl.multiple_of(i * tile, 16)
            here = pl.ds(at, tile)
            num = den = None
            for (ha, hb, d, kind, w), (h_spot, a_col, w_row_spot, w_col_spot) in zip(parts, spots):
                row = pl.multiple_of(offs[h_spot] + at, 16)
                w_row = pl.multiple_of(offs[w_row_spot] + at, 16)
                w_col = pl.multiple_of(offs[w_col_spot + j], BLK)
                weight = jnp.full((tile, BLK), fisher_floor, F32)
                for h, h_col, tok in zip((ha, hb), (a_col, 0), toks):
                    for e in range(2):
                        there = pl.ds(pl.multiple_of(tok + e * LEN, LEN), LEN)
                        grad = jnp.dot(
                            h[pl.ds(row, tile), h_col + e * LEN : h_col + (e + 1) * LEN],
                            d[j][there, :] if kind is None else d[j][kind, there, :],
                            preferred_element_type=F32,
                        )
                        weight = weight + grad * grad
                term = weight * w[pl.ds(w_row, tile), pl.ds(w_col, BLK)].astype(F32)
                num = term if num is None else num + term
                den = weight if den is None else den + weight
            for ref in recv:
                num = num + ref[0, here, cols].astype(F32)
                den = den + ref[1, here, cols].astype(F32)
            if final:
                out[here, cols] = (num / den).astype(BF)
            else:
                out[0, here, cols] = num.astype(BF)
                out[1, here, cols] = den.astype(BF)


def terms(offs, sources, rows, recv, final, before):
    nb = len(sources[0][2])
    wide = nb * BLK
    operands = [offs]
    for ha, hb, d, kind, w, spots in sources:
        operands += [ha, hb, *d, w]
    operands += [*recv, *before]
    return pl.pallas_call(
        functools.partial(term_kernel, rows, nb, [s[5] for s in sources], [s[3] for s in sources], len(recv), final),
        in_specs=[SMEM] + [VMEM] * (len(operands) - 1),
        out_specs=[VMEM, VMEM],
        out_shape=[jax.ShapeDtypeStruct((rows, wide) if final else (2, rows, wide), BF), TOKEN],
        compiler_params=pltpu.CompilerParams(vmem_limit_bytes=6 * 2**20),
        cost_estimate=FREE,
    )(*operands)


def merge_kernel(a, b, before, out, token):
    token[...] = jnp.zeros_like(token)
    num = a[0].astype(F32) + b[0].astype(F32)
    den = a[1].astype(F32) + b[1].astype(F32)
    out[...] = (num / den).astype(BF)


def merge(a, b, token):
    return pl.pallas_call(
        merge_kernel,
        in_specs=[VMEM] * 3,
        out_specs=[VMEM, VMEM],
        out_shape=[jax.ShapeDtypeStruct(a.shape[1:], BF), TOKEN],
        compiler_params=pltpu.CompilerParams(vmem_limit_bytes=6 * 2**20),
        cost_estimate=FREE,
    )(a, b, token)


def place_kernel(plan, n_parts, offs, *refs):
    parts, out, sem = refs[:n_parts], refs[-2], refs[-1]
    copies = []
    for part, lead, rows, row_at, col_at, nb in plan:
        src = parts[part] if lead is None else parts[part].at[lead]
        row = pl.multiple_of(offs[row_at], 16)
        for j in range(nb):
            col = pl.multiple_of(offs[col_at + j], BLK)
            copy = pltpu.make_async_copy(
                src.at[:, pl.ds(j * BLK, BLK)], out.at[pl.ds(row, rows), pl.ds(col, BLK)], sem.at[len(copies)]
            )
            copy.start()
            copies.append(copy)
    for copy in copies:
        copy.wait()


def place(shape, offs, parts, plan, before):
    return pl.pallas_call(
        functools.partial(place_kernel, plan, len(parts)),
        in_specs=[SMEM] + [VMEM] * (len(parts) + len(before)),
        out_specs=HBM,
        out_shape=jax.ShapeDtypeStruct(shape, BF),
        scratch_shapes=[pltpu.SemaphoreType.DMA((sum(p[-1] for p in plan),))],
        compiler_params=pltpu.CompilerParams(vmem_limit_bytes=2**20),
        cost_estimate=FREE,
    )(offs, *parts, *before)


def in_hbm(x):
    return pltpu.with_memory_space_constraint(x, pltpu.HBM)


def ints(*values):
    return jnp.stack([jnp.asarray(v, jnp.int32) for v in values])


def body(inputs, gate_weight, up_weight, cotangent, down_weight):
    task, core, col = lax.axis_index("task"), lax.axis_index("row"), lax.axis_index("col")
    y, h = task // 2, task % 2
    z_lo, x = col // 4, col % 4
    ring = 1 - 2 * core
    width, wide = down_weight.shape[1:]
    half, quarter, part = width // 2, width // 4, width // 8
    table = [core, (1 - h) * half, (1 - z_lo) * (wide // 2)]
    block = [(x - n) % 4 * BLK for n in range(4)]
    NEAR = len(table)
    table += [z_lo * (wide // 2) + b for b in block]
    FAR = len(table)
    table += [(1 - z_lo) * (wide // 2) + b for b in block]
    ALONE = len(table)
    table += block
    RING_ROW = len(table)
    table += [(y - k * ring) % 4 * quarter for k in range(4)]
    PART = len(table)
    table += [(y - k * ring) % 4 * part for k in range(4)]
    HERE = len(table)
    table += [h * half + (y - k * ring) % 4 * part for k in range(4)]
    BACK = len(table)
    table += [(y - k * ring) % 4 * quarter for k in range(4)]
    BACK_HERE = len(table)
    table += [h * half + (y - k * ring) % 4 * part for k in range(4)]
    BACK_AWAY = len(table)
    table += [(1 - h) * half + (y - k * ring) % 4 * part for k in range(4)]
    offs = ints(*table)

    mine = cotangent[0]
    near = [mine] + [move(mine, x_shift(n), "col") for n in (1, 2, 3)]
    far_mine = [move(mine, ZLO_SWAP, "col"), move(mine, Z_MIRROR, ("task", "col"))]
    w = down_weight[0]
    own, send, token = project(offs, inputs[0], gate_weight[0], up_weight[0])
    send, token = hold(send, [token, *near[1:], *far_mine])
    ha, away, far_pair, token = make_hidden(offs, own, move(send, CORE_SWAP, "row"), w, far_mine, [token])
    hb = move(ha, CORE_SWAP, "row")
    far = [far_pair] + [move(far_pair, x_shift(n), "col") for n in (1, 2, 3)]
    za = move(away, Z_SWAP)

    def ring_terms(p, k, recv, *before):
        at = RING_ROW + k
        d = near[2 * p : 2 * p + 2]
        return terms(offs, [(ha, hb, d, None, w, (at, 0, at, NEAR + 2 * p))], quarter, recv, False, before)

    def far_terms(k, recv, final, *before):
        return terms(
            offs,
            [
                (ha, hb, far, 0, w, (HERE + k, 0, HERE + k, FAR)),
                (za, zb, far, 1, za, (PART + k, wide // 2, PART + k, ALONE)),
            ],
            part, recv, final, before,
        )

    def around(piece):
        pieces = [piece]
        for _ in range(3):
            pieces.append(move(pieces[-1], RING, ("task", "row")))
        return pieces

    got = [(), ()]
    for k in (1, 2, 3):
        for p in range(2):
            extra = {(2, 1): far[1:2], (3, 0): far[3:4], (3, 1): far[2:3]}.get((k, p), [])
            piece, token = ring_terms(p, k, got[p], token, *extra)
            got[p] = (move(piece, RING, ("task", "row")),)
    zb, token = cut(za, HALF, token)
    zb = move(zb, CORE_SWAP, "row")
    a_sum, a_got, a_all = [None, None], [None, None], [None, None]
    a_sum[0], token = ring_terms(0, 0, got[0], token)
    a_got[0] = move(a_sum[0], Z_SWAP)
    b_got = ()
    for k in (1, 2, 3):
        piece, token = far_terms(k, b_got, False, token)
        b_got = (move(piece, RING, ("task", "row")),)
        if k == 1:
            a_sum[1], token = ring_terms(1, 0, got[1], token)
            a_got[1] = move(a_sum[1], Z_SWAP)
        if k == 2:
            out, token = merge(a_sum[0], a_got[0], token)
            a_all[0] = around(out)
        if k == 3:
            out, token = merge(a_sum[1], a_got[1], token)
            a_all[1] = around(out)
    b_out, token = far_terms(0, b_got, True, token)
    b_near = around(b_out)
    b_far = [move(piece, Z_SWAP) for piece in b_near]

    plan = []
    for k in range(4):
        plan += [(4 * p + k, None, quarter, BACK + k, NEAR + 2 * p, 2) for p in range(2)]
        plan += [(8 + k, None, part, BACK_HERE + k, FAR, 4), (12 + k, None, part, BACK_AWAY + k, FAR, 4)]
    return place((width, wide), offs, [*a_all[0], *a_all[1], *b_near, *b_far], plan, [token])


def solution(mesh):
    placed = (
        P("task", None, "row"),
        P("task", "row", "col"),
        P("task", "row", "col"),
        P("task", None, ("row", "col")),
        P("task", "col", "row"),
    )
    return jax.shard_map(
        body, mesh=mesh, in_specs=placed, out_specs=P("col", "row"), check_vma=False
    )
```

```python
import functools

import jax
import jax.numpy as jnp
from jax import lax
from jax.experimental import pallas as pl
from jax.experimental.pallas import tpu as pltpu
from jax.sharding import PartitionSpec as P

LEN = 128
HALF = 256
BLK = 256
fisher_floor = 0.05
F32 = jnp.float32
BF = jnp.bfloat16
VMEM = pl.BlockSpec(memory_space=pltpu.VMEM)
SMEM = pl.BlockSpec(memory_space=pltpu.SMEM)
ANY = pl.BlockSpec(memory_space=pl.ANY)
HBM = pl.BlockSpec(memory_space=pltpu.HBM)
TOKEN = jax.ShapeDtypeStruct((8, 128), F32)
FREE = pl.CostEstimate(flops=0, bytes_accessed=0, transcendentals=0)


def task_of(y, h):
    return y * 2 + h


def y_shift(n):
    return [(task_of(y, h), task_of((y + n) % 4, h)) for y in range(4) for h in range(2)]


def x_shift(n):
    return [(z * 4 + x, z * 4 + (x + n) % 4) for z in range(2) for x in range(4)]


Z_SWAP = [(task_of(y, h), task_of(y, 1 - h)) for y in range(4) for h in range(2)]
ZLO_SWAP = [(c, (c + 4) % 8) for c in range(8)]
CORE_SWAP = [(0, 1), (1, 0)]
X_GROUPS = [[z * 4 + x for x in range(4)] for z in range(2)]
Z_MIRROR = [
    (task_of(y, h) * 8 + c, task_of(y, 1 - h) * 8 + (c + 4) % 8) for y in range(4) for h in range(2) for c in range(8)
]
RING = [
    (task_of(y, h) * 2 + r, task_of((y + (1 if r == 0 else -1)) % 4, h) * 2 + r)
    for y in range(4)
    for h in range(2)
    for r in range(2)
]


def move(x, perm, axis="task"):
    return lax.ppermute(x, axis, perm)


def project_kernel(step, offs, x_hbm, g_hbm, u_hbm, own_ref, send_ref, token, x_ref, p_ref, sum_ref, sem):
    depth, width = g_hbm.shape
    steps = depth // step
    copies = []

    def fetch(src, dst):
        copy = pltpu.make_async_copy(src, dst, sem.at[len(copies)])
        copy.start()
        copies.append(copy)

    for half, side in enumerate((offs[0], 1 - offs[0])):
        rows = pl.ds(pl.multiple_of(side * HALF, HALF), HALF)
        fetch(x_hbm.at[rows, :], x_ref.at[pl.ds(half * HALF, HALF), :])
    for n in range(steps):
        for i, hbm in enumerate((g_hbm, u_hbm)):
            fetch(hbm.at[pl.ds(n * step, step), :], p_ref.at[i, pl.ds(n * step, step), :])
    token[...] = jnp.zeros_like(token)
    copies[0].wait()
    copies[1].wait()
    for n in range(steps):
        deep = pl.ds(n * step, step)
        for i in range(2):
            copies[2 + 2 * n + i].wait()
            for c in range(width // BLK):
                cols = pl.ds(c * BLK, BLK)
                both = jnp.dot(x_ref[:, deep], p_ref[i, deep, cols], preferred_element_type=F32)
                mine, other = both[:HALF], both[HALF:]
                if n > 0:
                    mine = mine + own_ref[i, :, cols]
                    other = other + sum_ref[i, :, cols]
                own_ref[i, :, cols] = mine
                if n < steps - 1:
                    sum_ref[i, :, cols] = other
                else:
                    send_ref[i, :, cols] = other.astype(BF)


def project(offs, x, w_gate, w_up):
    depth, width = w_gate.shape
    step = 512
    return pl.pallas_call(
        functools.partial(project_kernel, step),
        in_specs=[SMEM] + [HBM] * 3,
        out_specs=[VMEM] * 3,
        out_shape=[
            jax.ShapeDtypeStruct((2, HALF, width), F32),
            jax.ShapeDtypeStruct((2, HALF, width), BF),
            TOKEN,
        ],
        scratch_shapes=[
            pltpu.VMEM(x.shape, BF),
            pltpu.VMEM((2, depth, width), BF),
            pltpu.VMEM((2, HALF, width), F32),
            pltpu.SemaphoreType.DMA((2 + 2 * (depth // step),)),
        ],
        compiler_params=pltpu.CompilerParams(vmem_limit_bytes=22 * 2**20),
        cost_estimate=FREE,
    )(offs, in_hbm(x), in_hbm(w_gate), in_hbm(w_up))


def pass_kernel(n, *refs):
    refs[-1][...] = jnp.zeros_like(refs[-1])


def hold(x, before):
    return pl.pallas_call(
        functools.partial(pass_kernel, len(before)),
        in_specs=[VMEM] * (1 + len(before)),
        out_specs=[VMEM, VMEM],
        out_shape=[jax.ShapeDtypeStruct(x.shape, x.dtype), TOKEN],
        input_output_aliases={0: 0},
        compiler_params=pltpu.CompilerParams(vmem_limit_bytes=2**20),
        cost_estimate=FREE,
    )(x, *before)


def hidden_kernel(offs, own_ref, recv_ref, w_ref, c0_ref, c1_ref, *refs):
    out_ref, away_ref, pair_ref, token = refs[-4:]
    token[...] = jnp.zeros_like(token)
    step = 256
    for n in range(out_ref.shape[0] // step):
        cols = pl.ds(n * step, step)
        gate = own_ref[0, :, cols] + recv_ref[0, :, cols].astype(F32)
        up = own_ref[1, :, cols] + recv_ref[1, :, cols].astype(F32)
        hidden = jax.nn.gelu(gate, approximate=True) * up
        out_ref[cols, :] = hidden.T.astype(BF)
    half, wide = away_ref.shape
    wide -= HALF
    rows = pl.ds(pl.multiple_of(offs[1], 16), half)
    away_ref[:, wide:] = out_ref[rows, :]
    away_ref[:, :wide] = w_ref[rows, pl.ds(pl.multiple_of(offs[2], BLK), wide)]
    pair_ref[0] = c0_ref[...]
    pair_ref[1] = c1_ref[...]


def make_hidden(offs, own, recv, w, pair, before):
    width = own.shape[2]
    return pl.pallas_call(
        hidden_kernel,
        in_specs=[SMEM] + [VMEM] * (5 + len(before)),
        out_specs=[VMEM] * 4,
        out_shape=[
            jax.ShapeDtypeStruct((width, HALF), BF),
            jax.ShapeDtypeStruct((w.shape[0] // 2, w.shape[1] // 2 + HALF), BF),
            jax.ShapeDtypeStruct((2, *pair[0].shape), BF),
            TOKEN,
        ],
        compiler_params=pltpu.CompilerParams(vmem_limit_bytes=6 * 2**20),
        cost_estimate=FREE,
    )(offs, own, recv, w, *pair, *before)


def cut_kernel(a_ref, before, out_ref, token):
    token[...] = jnp.zeros_like(token)
    out_ref[...] = a_ref[:, a_ref.shape[1] - out_ref.shape[1] :]


def cut(a, wide, token):
    return pl.pallas_call(
        cut_kernel,
        in_specs=[VMEM, VMEM],
        out_specs=[VMEM, VMEM],
        out_shape=[jax.ShapeDtypeStruct((a.shape[0], wide), BF), TOKEN],
        compiler_params=pltpu.CompilerParams(vmem_limit_bytes=6 * 2**20),
        cost_estimate=FREE,
    )(a, token)


def term_kernel(rows, nb, spots, kinds, n_recv, final, offs, *refs):
    refs = list(refs)
    parts = []
    for kind in kinds:
        ha, hb, d = refs.pop(0), refs.pop(0), [refs.pop(0) for _ in range(nb)]
        parts.append((ha, hb, d, kind, refs.pop(0)))
    recv = [refs.pop(0) for _ in range(n_recv)]
    out, token = refs[-2:]
    token[...] = jnp.zeros_like(token)
    tile = next(t for t in (160, 128, 112, 96, 80, 64, 48, 32, 16) if rows % t == 0)
    toks = (offs[0] * HALF, (1 - offs[0]) * HALF)
    for j in range(nb):
        cols = pl.ds(j * BLK, BLK)

        @pl.loop(0, rows // tile)
        def _(i):
            at = pl.multiple_of(i * tile, 16)
            here = pl.ds(at, tile)
            num = den = None
            for (ha, hb, d, kind, w), (h_spot, a_col, w_row_spot, w_col_spot) in zip(parts, spots):
                row = pl.multiple_of(offs[h_spot] + at, 16)
                w_row = pl.multiple_of(offs[w_row_spot] + at, 16)
                w_col = pl.multiple_of(offs[w_col_spot + j], BLK)
                weight = jnp.full((tile, BLK), fisher_floor, F32)
                for h, h_col, tok in zip((ha, hb), (a_col, 0), toks):
                    for e in range(2):
                        there = pl.ds(pl.multiple_of(tok + e * LEN, LEN), LEN)
                        grad = jnp.dot(
                            h[pl.ds(row, tile), h_col + e * LEN : h_col + (e + 1) * LEN],
                            d[j][there, :] if kind is None else d[j][kind, there, :],
                            preferred_element_type=F32,
                        )
                        weight = weight + grad * grad
                term = weight * w[pl.ds(w_row, tile), pl.ds(w_col, BLK)].astype(F32)
                num = term if num is None else num + term
                den = weight if den is None else den + weight
            for ref in recv:
                num = num + ref[0, here, cols].astype(F32)
                den = den + ref[1, here, cols].astype(F32)
            if final:
                out[here, cols] = (num / den).astype(BF)
            else:
                out[0, here, cols] = num.astype(BF)
                out[1, here, cols] = den.astype(BF)


def terms(offs, sources, rows, recv, final, before):
    nb = len(sources[0][2])
    wide = nb * BLK
    operands = [offs]
    for ha, hb, d, kind, w, spots in sources:
        operands += [ha, hb, *d, w]
    operands += [*recv, *before]
    return pl.pallas_call(
        functools.partial(term_kernel, rows, nb, [s[5] for s in sources], [s[3] for s in sources], len(recv), final),
        in_specs=[SMEM] + [VMEM] * (len(operands) - 1),
        out_specs=[VMEM, VMEM],
        out_shape=[jax.ShapeDtypeStruct((rows, wide) if final else (2, rows, wide), BF), TOKEN],
        compiler_params=pltpu.CompilerParams(vmem_limit_bytes=6 * 2**20),
        cost_estimate=FREE,
    )(*operands)


def merge_kernel(a, b, before, out, token):
    token[...] = jnp.zeros_like(token)
    num = a[0].astype(F32) + b[0].astype(F32)
    den = a[1].astype(F32) + b[1].astype(F32)
    out[...] = (num / den).astype(BF)


def merge(a, b, token):
    return pl.pallas_call(
        merge_kernel,
        in_specs=[VMEM] * 3,
        out_specs=[VMEM, VMEM],
        out_shape=[jax.ShapeDtypeStruct(a.shape[1:], BF), TOKEN],
        compiler_params=pltpu.CompilerParams(vmem_limit_bytes=6 * 2**20),
        cost_estimate=FREE,
    )(a, b, token)


def place_kernel(plan, n_parts, offs, *refs):
    parts, out, sem = refs[:n_parts], refs[-2], refs[-1]
    copies = []
    for part, lead, rows, row_at, col_at, nb in plan:
        src = parts[part] if lead is None else parts[part].at[lead]
        row = pl.multiple_of(offs[row_at], 16)
        for j in range(nb):
            col = pl.multiple_of(offs[col_at + j], BLK)
            copy = pltpu.make_async_copy(
                src.at[:, pl.ds(j * BLK, BLK)], out.at[pl.ds(row, rows), pl.ds(col, BLK)], sem.at[len(copies)]
            )
            copy.start()
            copies.append(copy)
    for copy in copies:
        copy.wait()


def place(shape, offs, parts, plan, before):
    return pl.pallas_call(
        functools.partial(place_kernel, plan, len(parts)),
        in_specs=[SMEM] + [VMEM] * (len(parts) + len(before)),
        out_specs=HBM,
        out_shape=jax.ShapeDtypeStruct(shape, BF),
        scratch_shapes=[pltpu.SemaphoreType.DMA((sum(p[-1] for p in plan),))],
        compiler_params=pltpu.CompilerParams(vmem_limit_bytes=2**20),
        cost_estimate=FREE,
    )(offs, *parts, *before)


def in_hbm(x):
    return pltpu.with_memory_space_constraint(x, pltpu.HBM)


def ints(*values):
    return jnp.stack([jnp.asarray(v, jnp.int32) for v in values])


def body(inputs, gate_weight, up_weight, cotangent, down_weight):
    task, core, col = lax.axis_index("task"), lax.axis_index("row"), lax.axis_index("col")
    y, h = task // 2, task % 2
    z_lo, x = col // 4, col % 4
    ring = 1 - 2 * core
    width, wide = down_weight.shape[1:]
    half, quarter, part = width // 2, width // 4, width // 8
    table = [core, (1 - h) * half, (1 - z_lo) * (wide // 2)]
    block = [(x - n) % 4 * BLK for n in range(4)]
    NEAR = len(table)
    table += [z_lo * (wide // 2) + b for b in block]
    FAR = len(table)
    table += [(1 - z_lo) * (wide // 2) + b for b in block]
    ALONE = len(table)
    table += block
    RING_ROW = len(table)
    table += [(y - k * ring) % 4 * quarter for k in range(4)]
    PART = len(table)
    table += [(y - k * ring) % 4 * part for k in range(4)]
    HERE = len(table)
    table += [h * half + (y - k * ring) % 4 * part for k in range(4)]
    BACK = len(table)
    table += [(y - k * ring) % 4 * quarter for k in range(4)]
    BACK_HERE = len(table)
    table += [h * half + (y - k * ring) % 4 * part for k in range(4)]
    BACK_AWAY = len(table)
    table += [(1 - h) * half + (y - k * ring) % 4 * part for k in range(4)]
    offs = ints(*table)

    mine = cotangent[0]
    near = [mine] + [move(mine, x_shift(n), "col") for n in (1, 2, 3)]
    far_mine = [move(mine, ZLO_SWAP, "col"), move(mine, Z_MIRROR, ("task", "col"))]
    w = down_weight[0]
    own, send, token = project(offs, inputs[0], gate_weight[0], up_weight[0])
    send, token = hold(send, [token, *far_mine, near[1], near[3], near[2]])
    ha, away, far_pair, token = make_hidden(offs, own, move(send, CORE_SWAP, "row"), w, far_mine, [token])
    hb = move(ha, CORE_SWAP, "row")
    far = [far_pair] + [move(far_pair, x_shift(n), "col") for n in (1, 2, 3)]
    za = move(away, Z_SWAP)

    def ring_terms(p, k, recv, *before):
        at = RING_ROW + k
        d = near[2 * p : 2 * p + 2]
        return terms(offs, [(ha, hb, d, None, w, (at, 0, at, NEAR + 2 * p))], quarter, recv, False, before)

    def far_terms(k, recv, final, *before):
        return terms(
            offs,
            [
                (ha, hb, far, 0, w, (HERE + k, 0, HERE + k, FAR)),
                (za, zb, far, 1, za, (PART + k, wide // 2, PART + k, ALONE)),
            ],
            part, recv, final, before,
        )

    def onward(piece):
        return move(piece, RING, ("task", "row"))

    got = [(), ()]
    for k in (1, 2, 3):
        for p in range(2):
            extra = {(2, 1): [far[1], far[3]], (3, 1): far[2:3]}.get((k, p), [])
            piece, token = ring_terms(p, k, got[p], token, *extra)
            got[p] = (move(piece, RING, ("task", "row")),)
    zb, token = cut(za, HALF, token)
    zb = move(zb, CORE_SWAP, "row")
    a_sum, a_got, a_all = [None, None], [None, None], [None, None]
    a_sum[0], token = ring_terms(0, 0, got[0], token)
    a_got[0] = move(a_sum[0], Z_SWAP)
    b_got, early = (), []
    for k in (1, 2, 3):
        piece, token = far_terms(k, b_got, False, token)
        b_got = (onward(piece),)
        if k == 1:
            a_sum[1], token = ring_terms(1, 0, got[1], token)
            a_got[1] = move(a_sum[1], Z_SWAP)
        if k == 2:
            out, token = merge(a_sum[0], a_got[0], token)
            a_all[0] = [out, onward(out)]
            early = [a_all[0][1]]
        if k == 3:
            a_all[0].append(onward(a_all[0][1]))
            out, token = merge(a_sum[1], a_got[1], token)
            a_all[1] = [out, onward(out)]
    b_out, token = far_terms(0, b_got, True, token)
    a_all[0].append(onward(a_all[0][2]))
    b_near = [b_out, onward(b_out)]
    b_far = [move(piece, Z_SWAP) for piece in b_near]
    b_near.append(onward(b_near[1]))
    a_all[1].append(onward(a_all[1][1]))
    b_near[2], _ = hold(b_near[2], [b_far[0]])
    b_near.append(onward(b_near[2]))
    a_all[1][2], _ = hold(a_all[1][2], [b_far[1]])
    a_all[1].append(onward(a_all[1][2]))
    b_far += [move(piece, Z_SWAP) for piece in b_near[2:]]

    plan = []
    for k in range(4):
        plan += [(4 * p + k, None, quarter, BACK + k, NEAR + 2 * p, 2) for p in range(2)]
        plan += [(8 + k, None, part, BACK_HERE + k, FAR, 4), (12 + k, None, part, BACK_AWAY + k, FAR, 4)]
    return place((width, wide), offs, [*a_all[0], *a_all[1], *b_near, *b_far], plan, [token])


def solution(mesh):
    placed = (
        P("task", None, "row"),
        P("task", "row", "col"),
        P("task", "row", "col"),
        P("task", None, ("row", "col")),
        P("task", "col", "row"),
    )
    return jax.shard_map(
        body, mesh=mesh, in_specs=placed, out_specs=P("col", "row"), check_vma=False
    )
```

```python
import functools

import jax
import jax.numpy as jnp
from jax import lax
from jax.experimental import pallas as pl
from jax.experimental.pallas import tpu as pltpu
from jax.sharding import PartitionSpec as P

LEN = 128
HALF = 256
BLK = 256
fisher_floor = 0.05
F32 = jnp.float32
BF = jnp.bfloat16
VMEM = pl.BlockSpec(memory_space=pltpu.VMEM)
SMEM = pl.BlockSpec(memory_space=pltpu.SMEM)
ANY = pl.BlockSpec(memory_space=pl.ANY)
HBM = pl.BlockSpec(memory_space=pltpu.HBM)
TOKEN = jax.ShapeDtypeStruct((8, 128), F32)
FREE = pl.CostEstimate(flops=0, bytes_accessed=0, transcendentals=0)


def task_of(y, h):
    return y * 2 + h


def y_shift(n):
    return [(task_of(y, h), task_of((y + n) % 4, h)) for y in range(4) for h in range(2)]


def x_shift(n):
    return [(z * 4 + x, z * 4 + (x + n) % 4) for z in range(2) for x in range(4)]


Z_SWAP = [(task_of(y, h), task_of(y, 1 - h)) for y in range(4) for h in range(2)]
ZLO_SWAP = [(c, (c + 4) % 8) for c in range(8)]
CORE_SWAP = [(0, 1), (1, 0)]
X_GROUPS = [[z * 4 + x for x in range(4)] for z in range(2)]
Z_MIRROR = [
    (task_of(y, h) * 8 + c, task_of(y, 1 - h) * 8 + (c + 4) % 8) for y in range(4) for h in range(2) for c in range(8)
]
RING = [
    (task_of(y, h) * 2 + r, task_of((y + (1 if r == 0 else -1)) % 4, h) * 2 + r)
    for y in range(4)
    for h in range(2)
    for r in range(2)
]


def move(x, perm, axis="task"):
    return lax.ppermute(x, axis, perm)


def project_kernel(step, offs, x_hbm, g_hbm, u_hbm, own_ref, send_ref, token, x_ref, p_ref, sum_ref, sem):
    depth, width = g_hbm.shape
    steps = depth // step
    copies = []

    def fetch(src, dst):
        copy = pltpu.make_async_copy(src, dst, sem.at[len(copies)])
        copy.start()
        copies.append(copy)

    for half, side in enumerate((offs[0], 1 - offs[0])):
        rows = pl.ds(pl.multiple_of(side * HALF, HALF), HALF)
        fetch(x_hbm.at[rows, :], x_ref.at[pl.ds(half * HALF, HALF), :])
    for n in range(steps):
        for i, hbm in enumerate((g_hbm, u_hbm)):
            fetch(hbm.at[pl.ds(n * step, step), :], p_ref.at[i, pl.ds(n * step, step), :])
    token[...] = jnp.zeros_like(token)
    copies[0].wait()
    copies[1].wait()
    for n in range(steps):
        deep = pl.ds(n * step, step)
        for i in range(2):
            copies[2 + 2 * n + i].wait()
            for c in range(width // BLK):
                cols = pl.ds(c * BLK, BLK)
                both = jnp.dot(x_ref[:, deep], p_ref[i, deep, cols], preferred_element_type=F32)
                mine, other = both[:HALF], both[HALF:]
                if n > 0:
                    mine = mine + own_ref[i, :, cols]
                    other = other + sum_ref[i, :, cols]
                own_ref[i, :, cols] = mine
                if n < steps - 1:
                    sum_ref[i, :, cols] = other
                else:
                    send_ref[i, :, cols] = other.astype(BF)


def project(offs, x, w_gate, w_up):
    depth, width = w_gate.shape
    step = 512
    return pl.pallas_call(
        functools.partial(project_kernel, step),
        in_specs=[SMEM] + [HBM] * 3,
        out_specs=[VMEM] * 3,
        out_shape=[
            jax.ShapeDtypeStruct((2, HALF, width), F32),
            jax.ShapeDtypeStruct((2, HALF, width), BF),
            TOKEN,
        ],
        scratch_shapes=[
            pltpu.VMEM(x.shape, BF),
            pltpu.VMEM((2, depth, width), BF),
            pltpu.VMEM((2, HALF, width), F32),
            pltpu.SemaphoreType.DMA((2 + 2 * (depth // step),)),
        ],
        compiler_params=pltpu.CompilerParams(vmem_limit_bytes=22 * 2**20),
        cost_estimate=FREE,
    )(offs, in_hbm(x), in_hbm(w_gate), in_hbm(w_up))


def pass_kernel(n, *refs):
    refs[-1][...] = jnp.zeros_like(refs[-1])


def hold(x, before):
    return pl.pallas_call(
        functools.partial(pass_kernel, len(before)),
        in_specs=[VMEM] * (1 + len(before)),
        out_specs=[VMEM, VMEM],
        out_shape=[jax.ShapeDtypeStruct(x.shape, x.dtype), TOKEN],
        input_output_aliases={0: 0},
        compiler_params=pltpu.CompilerParams(vmem_limit_bytes=2**20),
        cost_estimate=FREE,
    )(x, *before)


def hidden_kernel(offs, own_ref, recv_ref, w_ref, c0_ref, c1_ref, *refs):
    out_ref, away_ref, pair_ref, token = refs[-4:]
    token[...] = jnp.zeros_like(token)
    step = 256
    for n in range(out_ref.shape[0] // step):
        cols = pl.ds(n * step, step)
        gate = own_ref[0, :, cols] + recv_ref[0, :, cols].astype(F32)
        up = own_ref[1, :, cols] + recv_ref[1, :, cols].astype(F32)
        hidden = jax.nn.gelu(gate, approximate=True) * up
        out_ref[cols, :] = hidden.T.astype(BF)
    half, wide = away_ref.shape
    wide -= HALF
    rows = pl.ds(pl.multiple_of(offs[1], 16), half)
    away_ref[:, wide:] = out_ref[rows, :]
    away_ref[:, :wide] = w_ref[rows, pl.ds(pl.multiple_of(offs[2], BLK), wide)]
    pair_ref[0] = c0_ref[...]
    pair_ref[1] = c1_ref[...]


def make_hidden(offs, own, recv, w, pair, before):
    width = own.shape[2]
    return pl.pallas_call(
        hidden_kernel,
        in_specs=[SMEM] + [VMEM] * (5 + len(before)),
        out_specs=[VMEM] * 4,
        out_shape=[
            jax.ShapeDtypeStruct((width, HALF), BF),
            jax.ShapeDtypeStruct((w.shape[0] // 2, w.shape[1] // 2 + HALF), BF),
            jax.ShapeDtypeStruct((2, *pair[0].shape), BF),
            TOKEN,
        ],
        compiler_params=pltpu.CompilerParams(vmem_limit_bytes=6 * 2**20),
        cost_estimate=FREE,
    )(offs, own, recv, w, *pair, *before)


def cut_kernel(a_ref, before, out_ref, token):
    token[...] = jnp.zeros_like(token)
    out_ref[...] = a_ref[:, a_ref.shape[1] - out_ref.shape[1] :]


def cut(a, wide, token):
    return pl.pallas_call(
        cut_kernel,
        in_specs=[VMEM, VMEM],
        out_specs=[VMEM, VMEM],
        out_shape=[jax.ShapeDtypeStruct((a.shape[0], wide), BF), TOKEN],
        compiler_params=pltpu.CompilerParams(vmem_limit_bytes=6 * 2**20),
        cost_estimate=FREE,
    )(a, token)


def term_kernel(rows, nb, spots, kinds, n_recv, final, offs, *refs):
    refs = list(refs)
    parts = []
    for kind in kinds:
        ha, hb, d = refs.pop(0), refs.pop(0), [refs.pop(0) for _ in range(nb)]
        parts.append((ha, hb, d, kind, refs.pop(0)))
    recv = [refs.pop(0) for _ in range(n_recv)]
    out, token = refs[-2:]
    token[...] = jnp.zeros_like(token)
    tile = next(t for t in (160, 128, 112, 96, 80, 64, 48, 32, 16) if rows % t == 0)
    toks = (offs[0] * HALF, (1 - offs[0]) * HALF)
    for j in range(nb):
        cols = pl.ds(j * BLK, BLK)

        @pl.loop(0, rows // tile)
        def _(i):
            at = pl.multiple_of(i * tile, 16)
            here = pl.ds(at, tile)
            num = den = None
            for (ha, hb, d, kind, w), (h_spot, a_col, w_row_spot, w_col_spot) in zip(parts, spots):
                row = pl.multiple_of(offs[h_spot] + at, 16)
                w_row = pl.multiple_of(offs[w_row_spot] + at, 16)
                w_col = pl.multiple_of(offs[w_col_spot + j], BLK)
                weight = jnp.full((tile, BLK), fisher_floor, F32)
                for h, h_col, tok in zip((ha, hb), (a_col, 0), toks):
                    for e in range(2):
                        there = pl.ds(pl.multiple_of(tok + e * LEN, LEN), LEN)
                        grad = jnp.dot(
                            h[pl.ds(row, tile), h_col + e * LEN : h_col + (e + 1) * LEN],
                            d[j][there, :] if kind is None else d[j][kind, there, :],
                            preferred_element_type=F32,
                        )
                        weight = weight + grad * grad
                term = weight * w[pl.ds(w_row, tile), pl.ds(w_col, BLK)].astype(F32)
                num = term if num is None else num + term
                den = weight if den is None else den + weight
            for ref in recv:
                num = num + ref[0, here, cols].astype(F32)
                den = den + ref[1, here, cols].astype(F32)
            if final:
                out[here, cols] = (num / den).astype(BF)
            else:
                out[0, here, cols] = num.astype(BF)
                out[1, here, cols] = den.astype(BF)


def terms(offs, sources, rows, recv, final, before):
    nb = len(sources[0][2])
    wide = nb * BLK
    operands = [offs]
    for ha, hb, d, kind, w, spots in sources:
        operands += [ha, hb, *d, w]
    operands += [*recv, *before]
    return pl.pallas_call(
        functools.partial(term_kernel, rows, nb, [s[5] for s in sources], [s[3] for s in sources], len(recv), final),
        in_specs=[SMEM] + [VMEM] * (len(operands) - 1),
        out_specs=[VMEM, VMEM],
        out_shape=[jax.ShapeDtypeStruct((rows, wide) if final else (2, rows, wide), BF), TOKEN],
        compiler_params=pltpu.CompilerParams(vmem_limit_bytes=6 * 2**20),
        cost_estimate=FREE,
    )(*operands)


def merge_kernel(a, b, before, out, token):
    token[...] = jnp.zeros_like(token)
    num = a[0].astype(F32) + b[0].astype(F32)
    den = a[1].astype(F32) + b[1].astype(F32)
    out[...] = (num / den).astype(BF)


def merge(a, b, token):
    return pl.pallas_call(
        merge_kernel,
        in_specs=[VMEM] * 3,
        out_specs=[VMEM, VMEM],
        out_shape=[jax.ShapeDtypeStruct(a.shape[1:], BF), TOKEN],
        compiler_params=pltpu.CompilerParams(vmem_limit_bytes=6 * 2**20),
        cost_estimate=FREE,
    )(a, b, token)


def place_kernel(plan, n_parts, offs, *refs):
    parts, out, sem = refs[:n_parts], refs[-2], refs[-1]
    copies = []
    for part, lead, rows, row_at, col_at, nb in plan:
        src = parts[part] if lead is None else parts[part].at[lead]
        row = pl.multiple_of(offs[row_at], 16)
        for j in range(nb):
            col = pl.multiple_of(offs[col_at + j], BLK)
            copy = pltpu.make_async_copy(
                src.at[:, pl.ds(j * BLK, BLK)], out.at[pl.ds(row, rows), pl.ds(col, BLK)], sem.at[len(copies)]
            )
            copy.start()
            copies.append(copy)
    for copy in copies:
        copy.wait()


def place(shape, offs, parts, plan, before):
    return pl.pallas_call(
        functools.partial(place_kernel, plan, len(parts)),
        in_specs=[SMEM] + [VMEM] * (len(parts) + len(before)),
        out_specs=HBM,
        out_shape=jax.ShapeDtypeStruct(shape, BF),
        scratch_shapes=[pltpu.SemaphoreType.DMA((sum(p[-1] for p in plan),))],
        compiler_params=pltpu.CompilerParams(vmem_limit_bytes=2**20),
        cost_estimate=FREE,
    )(offs, *parts, *before)


def in_hbm(x):
    return pltpu.with_memory_space_constraint(x, pltpu.HBM)


def ints(*values):
    return jnp.stack([jnp.asarray(v, jnp.int32) for v in values])


def body(inputs, gate_weight, up_weight, cotangent, down_weight):
    task, core, col = lax.axis_index("task"), lax.axis_index("row"), lax.axis_index("col")
    y, h = task // 2, task % 2
    z_lo, x = col // 4, col % 4
    ring = 1 - 2 * core
    width, wide = down_weight.shape[1:]
    half, quarter, part = width // 2, width // 4, width // 8
    table = [core, (1 - h) * half, (1 - z_lo) * (wide // 2)]
    block = [(x - n) % 4 * BLK for n in range(4)]
    NEAR = len(table)
    table += [z_lo * (wide // 2) + b for b in block]
    FAR = len(table)
    table += [(1 - z_lo) * (wide // 2) + b for b in block]
    ALONE = len(table)
    table += block
    RING_ROW = len(table)
    table += [(y - k * ring) % 4 * quarter for k in range(4)]
    PART = len(table)
    table += [(y - k * ring) % 4 * part for k in range(4)]
    HERE = len(table)
    table += [h * half + (y - k * ring) % 4 * part for k in range(4)]
    BACK = len(table)
    table += [(y - k * ring) % 4 * quarter for k in range(4)]
    BACK_HERE = len(table)
    table += [h * half + (y - k * ring) % 4 * part for k in range(4)]
    BACK_AWAY = len(table)
    table += [(1 - h) * half + (y - k * ring) % 4 * part for k in range(4)]
    offs = ints(*table)

    mine = cotangent[0]
    near = [mine] + [move(mine, x_shift(n), "col") for n in (1, 2, 3)]
    far_mine = [move(mine, ZLO_SWAP, "col"), move(mine, Z_MIRROR, ("task", "col"))]
    w = down_weight[0]
    own, send, token = project(offs, inputs[0], gate_weight[0], up_weight[0])
    send, token = hold(send, [token, *far_mine, near[1], near[3], near[2]])
    ha, away, far_pair, token = make_hidden(offs, own, move(send, CORE_SWAP, "row"), w, far_mine, [token])
    hb = move(ha, CORE_SWAP, "row")
    far = [far_pair] + [move(far_pair, x_shift(n), "col") for n in (1, 2, 3)]
    za = move(away, Z_SWAP)

    def ring_terms(p, k, recv, *before):
        at = RING_ROW + k
        d = near[2 * p : 2 * p + 2]
        return terms(offs, [(ha, hb, d, None, w, (at, 0, at, NEAR + 2 * p))], quarter, recv, False, before)

    def far_terms(k, recv, final, *before):
        return terms(
            offs,
            [
                (ha, hb, far, 0, w, (HERE + k, 0, HERE + k, FAR)),
                (za, zb, far, 1, za, (PART + k, wide // 2, PART + k, ALONE)),
            ],
            part, recv, final, before,
        )

    def onward(piece):
        return move(piece, RING, ("task", "row"))

    got = [(), ()]
    for k in (1, 2, 3):
        for p in range(2):
            extra = {(2, 1): [far[1], far[3]], (3, 1): far[2:3]}.get((k, p), [])
            piece, token = ring_terms(p, k, got[p], token, *extra)
            got[p] = (move(piece, RING, ("task", "row")),)
    a_sum, a_got, a_all = [None, None], [None, None], [None, None]
    a_sum[0], token = ring_terms(0, 0, got[0], token)
    a_got[0] = move(a_sum[0], Z_SWAP)
    zb, token = cut(za, HALF, token)
    zb = move(zb, CORE_SWAP, "row")
    b_got, early = (), []
    for k in (1, 2, 3):
        piece, token = far_terms(k, b_got, False, token)
        b_got = (onward(piece),)
        if k == 1:
            a_sum[1], token = ring_terms(1, 0, got[1], token)
            a_got[1] = move(a_sum[1], Z_SWAP)
        if k == 2:
            out, token = merge(a_sum[0], a_got[0], token)
            a_all[0] = [out, onward(out)]
            early = [a_all[0][1]]
        if k == 3:
            a_all[0].append(onward(a_all[0][1]))
            out, token = merge(a_sum[1], a_got[1], token)
            a_all[1] = [out, onward(out)]
    b_out, token = far_terms(0, b_got, True, token)
    a_all[0].append(onward(a_all[0][2]))
    b_near = [b_out, onward(b_out)]
    b_far = [move(piece, Z_SWAP) for piece in b_near]
    b_near.append(onward(b_near[1]))
    a_all[1].append(onward(a_all[1][1]))
    b_near[2], _ = hold(b_near[2], [b_far[0]])
    b_near.append(onward(b_near[2]))
    a_all[1][2], _ = hold(a_all[1][2], [b_far[1]])
    a_all[1].append(onward(a_all[1][2]))
    b_far += [move(piece, Z_SWAP) for piece in b_near[2:]]

    plan = []
    for k in range(4):
        plan += [(4 * p + k, None, quarter, BACK + k, NEAR + 2 * p, 2) for p in range(2)]
        plan += [(8 + k, None, part, BACK_HERE + k, FAR, 4), (12 + k, None, part, BACK_AWAY + k, FAR, 4)]
    return place((width, wide), offs, [*a_all[0], *a_all[1], *b_near, *b_far], plan, [token])


def solution(mesh):
    placed = (
        P("task", None, "row"),
        P("task", "row", "col"),
        P("task", "row", "col"),
        P("task", None, ("row", "col")),
        P("task", "col", "row"),
    )
    return jax.shard_map(
        body, mesh=mesh, in_specs=placed, out_specs=P("col", "row"), check_vma=False
    )
```

```python
import functools

import jax
import jax.numpy as jnp
from jax import lax
from jax.experimental import pallas as pl
from jax.experimental.pallas import tpu as pltpu
from jax.sharding import PartitionSpec as P

LEN = 128
HALF = 256
BLK = 256
fisher_floor = 0.05
F32 = jnp.float32
BF = jnp.bfloat16
VMEM = pl.BlockSpec(memory_space=pltpu.VMEM)
SMEM = pl.BlockSpec(memory_space=pltpu.SMEM)
ANY = pl.BlockSpec(memory_space=pl.ANY)
HBM = pl.BlockSpec(memory_space=pltpu.HBM)
TOKEN = jax.ShapeDtypeStruct((8, 128), F32)
FREE = pl.CostEstimate(flops=0, bytes_accessed=0, transcendentals=0)


def task_of(y, h):
    return y * 2 + h


def y_shift(n):
    return [(task_of(y, h), task_of((y + n) % 4, h)) for y in range(4) for h in range(2)]


def x_shift(n):
    return [(z * 4 + x, z * 4 + (x + n) % 4) for z in range(2) for x in range(4)]


Z_SWAP = [(task_of(y, h), task_of(y, 1 - h)) for y in range(4) for h in range(2)]
ZLO_SWAP = [(c, (c + 4) % 8) for c in range(8)]
CORE_SWAP = [(0, 1), (1, 0)]
X_GROUPS = [[z * 4 + x for x in range(4)] for z in range(2)]
Z_MIRROR = [
    (task_of(y, h) * 8 + c, task_of(y, 1 - h) * 8 + (c + 4) % 8) for y in range(4) for h in range(2) for c in range(8)
]
RING = [
    (task_of(y, h) * 2 + r, task_of((y + (1 if r == 0 else -1)) % 4, h) * 2 + r)
    for y in range(4)
    for h in range(2)
    for r in range(2)
]


def move(x, perm, axis="task"):
    return lax.ppermute(x, axis, perm)


def project_kernel(step, offs, x_hbm, g_hbm, u_hbm, own_ref, send_ref, token, x_ref, p_ref, sum_ref, sem):
    depth, width = g_hbm.shape
    steps = depth // step
    copies = []

    def fetch(src, dst):
        copy = pltpu.make_async_copy(src, dst, sem.at[len(copies)])
        copy.start()
        copies.append(copy)

    for half, side in enumerate((offs[0], 1 - offs[0])):
        rows = pl.ds(pl.multiple_of(side * HALF, HALF), HALF)
        fetch(x_hbm.at[rows, :], x_ref.at[pl.ds(half * HALF, HALF), :])
    for n in range(steps):
        for i, hbm in enumerate((g_hbm, u_hbm)):
            fetch(hbm.at[pl.ds(n * step, step), :], p_ref.at[i, pl.ds(n * step, step), :])
    token[...] = jnp.zeros_like(token)
    copies[0].wait()
    copies[1].wait()
    for n in range(steps):
        deep = pl.ds(n * step, step)
        for i in range(2):
            copies[2 + 2 * n + i].wait()
            for c in range(width // BLK):
                cols = pl.ds(c * BLK, BLK)
                both = jnp.dot(x_ref[:, deep], p_ref[i, deep, cols], preferred_element_type=F32)
                mine, other = both[:HALF], both[HALF:]
                if n > 0:
                    mine = mine + own_ref[i, :, cols]
                    other = other + sum_ref[i, :, cols]
                own_ref[i, :, cols] = mine
                if n < steps - 1:
                    sum_ref[i, :, cols] = other
                else:
                    send_ref[i, :, cols] = other.astype(BF)


def project(offs, x, w_gate, w_up):
    depth, width = w_gate.shape
    step = 512
    return pl.pallas_call(
        functools.partial(project_kernel, step),
        in_specs=[SMEM] + [HBM] * 3,
        out_specs=[VMEM] * 3,
        out_shape=[
            jax.ShapeDtypeStruct((2, HALF, width), F32),
            jax.ShapeDtypeStruct((2, HALF, width), BF),
            TOKEN,
        ],
        scratch_shapes=[
            pltpu.VMEM(x.shape, BF),
            pltpu.VMEM((2, depth, width), BF),
            pltpu.VMEM((2, HALF, width), F32),
            pltpu.SemaphoreType.DMA((2 + 2 * (depth // step),)),
        ],
        compiler_params=pltpu.CompilerParams(vmem_limit_bytes=22 * 2**20),
        cost_estimate=FREE,
    )(offs, in_hbm(x), in_hbm(w_gate), in_hbm(w_up))


def pass_kernel(n, *refs):
    refs[-1][...] = jnp.zeros_like(refs[-1])


def hold(x, before):
    return pl.pallas_call(
        functools.partial(pass_kernel, len(before)),
        in_specs=[VMEM] * (1 + len(before)),
        out_specs=[VMEM, VMEM],
        out_shape=[jax.ShapeDtypeStruct(x.shape, x.dtype), TOKEN],
        input_output_aliases={0: 0},
        compiler_params=pltpu.CompilerParams(vmem_limit_bytes=2**20),
        cost_estimate=FREE,
    )(x, *before)


def hidden_kernel(offs, own_ref, recv_ref, w_ref, c0_ref, c1_ref, *refs):
    out_ref, away_ref, pair_ref, token = refs[-4:]
    token[...] = jnp.zeros_like(token)
    step = 256
    for n in range(out_ref.shape[0] // step):
        cols = pl.ds(n * step, step)
        gate = own_ref[0, :, cols] + recv_ref[0, :, cols].astype(F32)
        up = own_ref[1, :, cols] + recv_ref[1, :, cols].astype(F32)
        hidden = jax.nn.gelu(gate, approximate=True) * up
        out_ref[cols, :] = hidden.T.astype(BF)
    half, wide = away_ref.shape
    wide -= HALF
    rows = pl.ds(pl.multiple_of(offs[1], 16), half)
    away_ref[:, wide:] = out_ref[rows, :]
    away_ref[:, :wide] = w_ref[rows, pl.ds(pl.multiple_of(offs[2], BLK), wide)]
    pair_ref[0] = c0_ref[...]
    pair_ref[1] = c1_ref[...]


def make_hidden(offs, own, recv, w, pair, before):
    width = own.shape[2]
    return pl.pallas_call(
        hidden_kernel,
        in_specs=[SMEM] + [VMEM] * (5 + len(before)),
        out_specs=[VMEM] * 4,
        out_shape=[
            jax.ShapeDtypeStruct((width, HALF), BF),
            jax.ShapeDtypeStruct((w.shape[0] // 2, w.shape[1] // 2 + HALF), BF),
            jax.ShapeDtypeStruct((2, *pair[0].shape), BF),
            TOKEN,
        ],
        compiler_params=pltpu.CompilerParams(vmem_limit_bytes=6 * 2**20),
        cost_estimate=FREE,
    )(offs, own, recv, w, *pair, *before)


def cut_kernel(a_ref, before, out_ref, token):
    token[...] = jnp.zeros_like(token)
    out_ref[...] = a_ref[:, a_ref.shape[1] - out_ref.shape[1] :]


def cut(a, wide, token):
    return pl.pallas_call(
        cut_kernel,
        in_specs=[VMEM, VMEM],
        out_specs=[VMEM, VMEM],
        out_shape=[jax.ShapeDtypeStruct((a.shape[0], wide), BF), TOKEN],
        compiler_params=pltpu.CompilerParams(vmem_limit_bytes=6 * 2**20),
        cost_estimate=FREE,
    )(a, token)


def term_kernel(rows, nb, spots, kinds, n_recv, final, offs, *refs):
    refs = list(refs)
    parts = []
    for kind in kinds:
        ha, hb, d = refs.pop(0), refs.pop(0), [refs.pop(0) for _ in range(nb)]
        parts.append((ha, hb, d, kind, refs.pop(0)))
    recv = [refs.pop(0) for _ in range(n_recv)]
    out, token = refs[-2:]
    token[...] = jnp.zeros_like(token)
    tile = next(t for t in (160, 128, 112, 96, 80, 64, 48, 32, 16) if rows % t == 0)
    toks = (offs[0] * HALF, (1 - offs[0]) * HALF)
    for j in range(nb):
        cols = pl.ds(j * BLK, BLK)

        @pl.loop(0, rows // tile)
        def _(i):
            at = pl.multiple_of(i * tile, 16)
            here = pl.ds(at, tile)
            num = den = None
            for (ha, hb, d, kind, w), (h_spot, a_col, w_row_spot, w_col_spot) in zip(parts, spots):
                row = pl.multiple_of(offs[h_spot] + at, 16)
                w_row = pl.multiple_of(offs[w_row_spot] + at, 16)
                w_col = pl.multiple_of(offs[w_col_spot + j], BLK)
                weight = jnp.full((tile, BLK), fisher_floor, F32)
                for h, h_col, tok in zip((ha, hb), (a_col, 0), toks):
                    for e in range(2):
                        there = pl.ds(pl.multiple_of(tok + e * LEN, LEN), LEN)
                        grad = jnp.dot(
                            h[pl.ds(row, tile), h_col + e * LEN : h_col + (e + 1) * LEN],
                            d[j][there, :] if kind is None else d[j][kind, there, :],
                            preferred_element_type=F32,
                        )
                        weight = weight + grad * grad
                term = weight * w[pl.ds(w_row, tile), pl.ds(w_col, BLK)].astype(F32)
                num = term if num is None else num + term
                den = weight if den is None else den + weight
            for ref in recv:
                num = num + ref[0, here, cols].astype(F32)
                den = den + ref[1, here, cols].astype(F32)
            if final:
                out[here, cols] = (num / den).astype(BF)
            else:
                out[0, here, cols] = num.astype(BF)
                out[1, here, cols] = den.astype(BF)


def terms(offs, sources, rows, recv, final, before):
    nb = len(sources[0][2])
    wide = nb * BLK
    operands = [offs]
    for ha, hb, d, kind, w, spots in sources:
        operands += [ha, hb, *d, w]
    operands += [*recv, *before]
    return pl.pallas_call(
        functools.partial(term_kernel, rows, nb, [s[5] for s in sources], [s[3] for s in sources], len(recv), final),
        in_specs=[SMEM] + [VMEM] * (len(operands) - 1),
        out_specs=[VMEM, VMEM],
        out_shape=[jax.ShapeDtypeStruct((rows, wide) if final else (2, rows, wide), BF), TOKEN],
        compiler_params=pltpu.CompilerParams(vmem_limit_bytes=6 * 2**20),
        cost_estimate=FREE,
    )(*operands)


def merge_kernel(a, b, before, out, token):
    token[...] = jnp.zeros_like(token)
    num = a[0].astype(F32) + b[0].astype(F32)
    den = a[1].astype(F32) + b[1].astype(F32)
    out[...] = (num / den).astype(BF)


def merge(a, b, token):
    return pl.pallas_call(
        merge_kernel,
        in_specs=[VMEM] * 3,
        out_specs=[VMEM, VMEM],
        out_shape=[jax.ShapeDtypeStruct(a.shape[1:], BF), TOKEN],
        compiler_params=pltpu.CompilerParams(vmem_limit_bytes=6 * 2**20),
        cost_estimate=FREE,
    )(a, b, token)


def place_kernel(plan, n_parts, offs, *refs):
    parts, (out, token, sem) = refs[:n_parts], refs[-3:]
    token[...] = jnp.zeros_like(token)
    copies = []
    for part, rows, row_at, col_at, nb in plan:
        row = pl.multiple_of(offs[row_at], 16)
        for j in range(nb):
            col = pl.multiple_of(offs[col_at + j], BLK)
            copy = pltpu.make_async_copy(
                parts[part].at[:, pl.ds(j * BLK, BLK)], out.at[pl.ds(row, rows), pl.ds(col, BLK)], sem.at[len(copies)]
            )
            copy.start()
            copies.append(copy)
    for copy in copies:
        copy.wait()


def place(shape, offs, pieces, into, before):
    parts = [piece[0] for piece in pieces]
    plan = [(n, piece[0].shape[0], *piece[1:]) for n, piece in enumerate(pieces)]
    operands = [offs, *parts, *before] + ([] if into is None else [into])
    last = len(operands) - 1
    return pl.pallas_call(
        functools.partial(place_kernel, plan, len(parts)),
        in_specs=[SMEM] + [VMEM] * (len(parts) + len(before)) + ([] if into is None else [HBM]),
        out_specs=[HBM, VMEM],
        out_shape=[jax.ShapeDtypeStruct(shape, BF), TOKEN],
        scratch_shapes=[pltpu.SemaphoreType.DMA((sum(p[-1] for p in plan),))],
        input_output_aliases={} if into is None else {last: 0},
        compiler_params=pltpu.CompilerParams(vmem_limit_bytes=2**20),
        cost_estimate=FREE,
    )(*operands)


def in_hbm(x):
    return pltpu.with_memory_space_constraint(x, pltpu.HBM)


def ints(*values):
    return jnp.stack([jnp.asarray(v, jnp.int32) for v in values])


def body(inputs, gate_weight, up_weight, cotangent, down_weight):
    task, core, col = lax.axis_index("task"), lax.axis_index("row"), lax.axis_index("col")
    y, h = task // 2, task % 2
    z_lo, x = col // 4, col % 4
    ring = 1 - 2 * core
    width, wide = down_weight.shape[1:]
    half, quarter, part = width // 2, width // 4, width // 8
    table = [core, (1 - h) * half, (1 - z_lo) * (wide // 2)]
    block = [(x - n) % 4 * BLK for n in range(4)]
    NEAR = len(table)
    table += [z_lo * (wide // 2) + b for b in block]
    FAR = len(table)
    table += [(1 - z_lo) * (wide // 2) + b for b in block]
    ALONE = len(table)
    table += block
    RING_ROW = len(table)
    table += [(y - k * ring) % 4 * quarter for k in range(4)]
    PART = len(table)
    table += [(y - k * ring) % 4 * part for k in range(4)]
    HERE = len(table)
    table += [h * half + (y - k * ring) % 4 * part for k in range(4)]
    BACK = len(table)
    table += [(y - k * ring) % 4 * quarter for k in range(4)]
    BACK_HERE = len(table)
    table += [h * half + (y - k * ring) % 4 * part for k in range(4)]
    BACK_AWAY = len(table)
    table += [(1 - h) * half + (y - k * ring) % 4 * part for k in range(4)]
    offs = ints(*table)

    mine = cotangent[0]
    near = [mine] + [move(mine, x_shift(n), "col") for n in (1, 2, 3)]
    far_mine = [move(mine, ZLO_SWAP, "col"), move(mine, Z_MIRROR, ("task", "col"))]
    w = down_weight[0]
    own, send, token = project(offs, inputs[0], gate_weight[0], up_weight[0])
    send, token = hold(send, [token, *far_mine, near[1], near[3], near[2]])
    ha, away, far_pair, token = make_hidden(offs, own, move(send, CORE_SWAP, "row"), w, far_mine, [token])
    hb = move(ha, CORE_SWAP, "row")
    far = [far_pair] + [move(far_pair, x_shift(n), "col") for n in (1, 2, 3)]
    za = move(away, Z_SWAP)

    def ring_terms(p, k, recv, *before):
        at = RING_ROW + k
        d = near[2 * p : 2 * p + 2]
        return terms(offs, [(ha, hb, d, None, w, (at, 0, at, NEAR + 2 * p))], quarter, recv, False, before)

    def far_terms(k, recv, final, *before):
        return terms(
            offs,
            [
                (ha, hb, far, 0, w, (HERE + k, 0, HERE + k, FAR)),
                (za, zb, far, 1, za, (PART + k, wide // 2, PART + k, ALONE)),
            ],
            part, recv, final, before,
        )

    def onward(piece):
        return move(piece, RING, ("task", "row"))

    got = [(), ()]
    for k in (1, 2, 3):
        for p in range(2):
            extra = {(2, 1): [far[1], far[3]], (3, 1): far[2:3]}.get((k, p), [])
            piece, token = ring_terms(p, k, got[p], token, *extra)
            got[p] = (move(piece, RING, ("task", "row")),)
    zb, token = cut(za, HALF, token)
    zb = move(zb, CORE_SWAP, "row")
    a_sum, a_got, a_all = [None, None], [None, None], [None, None]
    a_sum[0], token = ring_terms(0, 0, got[0], token)
    a_got[0] = move(a_sum[0], Z_SWAP)
    b_got, early = (), []
    for k in (1, 2, 3):
        piece, token = far_terms(k, b_got, False, token)
        b_got = (onward(piece),)
        if k == 1:
            a_sum[1], token = ring_terms(1, 0, got[1], token)
            a_got[1] = move(a_sum[1], Z_SWAP)
        if k == 2:
            out, token = merge(a_sum[0], a_got[0], token)
            a_all[0] = [out, onward(out)]
            early = [a_all[0][1]]
        if k == 3:
            a_all[0].append(onward(a_all[0][1]))
            out, token = merge(a_sum[1], a_got[1], token)
            a_all[1] = [out, onward(out)]
    b_out, token = far_terms(0, b_got, True, token)
    a_all[0].append(onward(a_all[0][2]))
    b_near = [b_out, onward(b_out)]
    b_far = [move(piece, Z_SWAP) for piece in b_near]
    b_near.append(onward(b_near[1]))
    a_all[1].append(onward(a_all[1][1]))
    b_near[2], _ = hold(b_near[2], [b_far[0]])
    b_near.append(onward(b_near[2]))

    def a_place(p, k):
        return a_all[p][k], BACK + k, NEAR + 2 * p, 2

    def b_place(k):
        return b_near[k], BACK_HERE + k, FAR, 4

    def b_place_far(k):
        return b_far[k], BACK_AWAY + k, FAR, 4

    shape = (width, wide)
    first = [a_place(0, 0), a_place(0, 1), a_place(1, 0), a_place(1, 1), b_place(0), b_place(1), b_place(2), b_place_far(0)]
    begun, done = place(shape, offs, first, None, [])
    a_all[1][2], _ = hold(a_all[1][2], [b_far[1], done])
    a_all[1].append(onward(a_all[1][2]))
    b_far += [move(piece, Z_SWAP) for piece in b_near[2:]]

    rest = [a_place(0, 2), a_place(0, 3), a_place(1, 2), a_place(1, 3), b_place(3)]
    rest += [b_place_far(k) for k in (1, 2, 3)]
    return place(shape, offs, rest, begun, [])[0]


def solution(mesh):
    placed = (
        P("task", None, "row"),
        P("task", "row", "col"),
        P("task", "row", "col"),
        P("task", None, ("row", "col")),
        P("task", "col", "row"),
    )
    return jax.shard_map(
        body, mesh=mesh, in_specs=placed, out_specs=P("col", "row"), check_vma=False
    )
```

```python
import functools

import jax
import jax.numpy as jnp
from jax import lax
from jax.experimental import pallas as pl
from jax.experimental.pallas import tpu as pltpu
from jax.sharding import PartitionSpec as P

LEN = 128
HALF = 256
BLK = 256
fisher_floor = 0.05
F32 = jnp.float32
BF = jnp.bfloat16
VMEM = pl.BlockSpec(memory_space=pltpu.VMEM)
SMEM = pl.BlockSpec(memory_space=pltpu.SMEM)
ANY = pl.BlockSpec(memory_space=pl.ANY)
HBM = pl.BlockSpec(memory_space=pltpu.HBM)
TOKEN = jax.ShapeDtypeStruct((8, 128), F32)
FREE = pl.CostEstimate(flops=0, bytes_accessed=0, transcendentals=0)


def task_of(y, h):
    return y * 2 + h


def y_shift(n):
    return [(task_of(y, h), task_of((y + n) % 4, h)) for y in range(4) for h in range(2)]


def x_shift(n):
    return [(z * 4 + x, z * 4 + (x + n) % 4) for z in range(2) for x in range(4)]


Z_SWAP = [(task_of(y, h), task_of(y, 1 - h)) for y in range(4) for h in range(2)]
ZLO_SWAP = [(c, (c + 4) % 8) for c in range(8)]
CORE_SWAP = [(0, 1), (1, 0)]
X_GROUPS = [[z * 4 + x for x in range(4)] for z in range(2)]
Z_MIRROR = [
    (task_of(y, h) * 8 + c, task_of(y, 1 - h) * 8 + (c + 4) % 8) for y in range(4) for h in range(2) for c in range(8)
]
RING = [
    (task_of(y, h) * 2 + r, task_of((y + (1 if r == 0 else -1)) % 4, h) * 2 + r)
    for y in range(4)
    for h in range(2)
    for r in range(2)
]


def move(x, perm, axis="task"):
    return lax.ppermute(x, axis, perm)


def project_kernel(step, offs, x_hbm, g_hbm, u_hbm, own_ref, send_ref, token, x_ref, p_ref, sum_ref, sem):
    depth, width = g_hbm.shape
    steps = depth // step
    copies = []

    def fetch(src, dst):
        copy = pltpu.make_async_copy(src, dst, sem.at[len(copies)])
        copy.start()
        copies.append(copy)

    for half, side in enumerate((offs[0], 1 - offs[0])):
        rows = pl.ds(pl.multiple_of(side * HALF, HALF), HALF)
        fetch(x_hbm.at[rows, :], x_ref.at[pl.ds(half * HALF, HALF), :])
    for n in range(steps):
        for i, hbm in enumerate((g_hbm, u_hbm)):
            fetch(hbm.at[pl.ds(n * step, step), :], p_ref.at[i, pl.ds(n * step, step), :])
    token[...] = jnp.zeros_like(token)
    copies[0].wait()
    copies[1].wait()
    for n in range(steps):
        deep = pl.ds(n * step, step)
        for i in range(2):
            copies[2 + 2 * n + i].wait()
            for c in range(width // BLK):
                cols = pl.ds(c * BLK, BLK)
                both = jnp.dot(x_ref[:, deep], p_ref[i, deep, cols], preferred_element_type=F32)
                mine, other = both[:HALF], both[HALF:]
                if n > 0:
                    mine = mine + own_ref[i, :, cols]
                    other = other + sum_ref[i, :, cols]
                own_ref[i, :, cols] = mine
                if n < steps - 1:
                    sum_ref[i, :, cols] = other
                else:
                    send_ref[i, :, cols] = other.astype(BF)


def project(offs, x, w_gate, w_up):
    depth, width = w_gate.shape
    step = 512
    return pl.pallas_call(
        functools.partial(project_kernel, step),
        in_specs=[SMEM] + [HBM] * 3,
        out_specs=[VMEM] * 3,
        out_shape=[
            jax.ShapeDtypeStruct((2, HALF, width), F32),
            jax.ShapeDtypeStruct((2, HALF, width), BF),
            TOKEN,
        ],
        scratch_shapes=[
            pltpu.VMEM(x.shape, BF),
            pltpu.VMEM((2, depth, width), BF),
            pltpu.VMEM((2, HALF, width), F32),
            pltpu.SemaphoreType.DMA((2 + 2 * (depth // step),)),
        ],
        compiler_params=pltpu.CompilerParams(vmem_limit_bytes=22 * 2**20),
        cost_estimate=FREE,
    )(offs, in_hbm(x), in_hbm(w_gate), in_hbm(w_up))


def pass_kernel(n, *refs):
    refs[-1][...] = jnp.zeros_like(refs[-1])


def hold(x, before):
    return pl.pallas_call(
        functools.partial(pass_kernel, len(before)),
        in_specs=[VMEM] * (1 + len(before)),
        out_specs=[VMEM, VMEM],
        out_shape=[jax.ShapeDtypeStruct(x.shape, x.dtype), TOKEN],
        input_output_aliases={0: 0},
        compiler_params=pltpu.CompilerParams(vmem_limit_bytes=2**20),
        cost_estimate=FREE,
    )(x, *before)


def hidden_kernel(offs, own_ref, recv_ref, w_ref, c0_ref, c1_ref, *refs):
    out_ref, away_ref, pair_ref, token = refs[-4:]
    token[...] = jnp.zeros_like(token)
    step = 256
    for n in range(out_ref.shape[0] // step):
        cols = pl.ds(n * step, step)
        gate = own_ref[0, :, cols] + recv_ref[0, :, cols].astype(F32)
        up = own_ref[1, :, cols] + recv_ref[1, :, cols].astype(F32)
        hidden = jax.nn.gelu(gate, approximate=True) * up
        out_ref[cols, :] = hidden.T.astype(BF)
    half, wide = away_ref.shape
    wide -= HALF
    rows = pl.ds(pl.multiple_of(offs[1], 16), half)
    away_ref[:, wide:] = out_ref[rows, :]
    away_ref[:, :wide] = w_ref[rows, pl.ds(pl.multiple_of(offs[2], BLK), wide)]
    pair_ref[0] = c0_ref[...]
    pair_ref[1] = c1_ref[...]


def make_hidden(offs, own, recv, w, pair, before):
    width = own.shape[2]
    return pl.pallas_call(
        hidden_kernel,
        in_specs=[SMEM] + [VMEM] * (5 + len(before)),
        out_specs=[VMEM] * 4,
        out_shape=[
            jax.ShapeDtypeStruct((width, HALF), BF),
            jax.ShapeDtypeStruct((w.shape[0] // 2, w.shape[1] // 2 + HALF), BF),
            jax.ShapeDtypeStruct((2, *pair[0].shape), BF),
            TOKEN,
        ],
        compiler_params=pltpu.CompilerParams(vmem_limit_bytes=6 * 2**20),
        cost_estimate=FREE,
    )(offs, own, recv, w, *pair, *before)


def cut_kernel(a_ref, before, out_ref, token):
    token[...] = jnp.zeros_like(token)
    out_ref[...] = a_ref[:, a_ref.shape[1] - out_ref.shape[1] :]


def cut(a, wide, token):
    return pl.pallas_call(
        cut_kernel,
        in_specs=[VMEM, VMEM],
        out_specs=[VMEM, VMEM],
        out_shape=[jax.ShapeDtypeStruct((a.shape[0], wide), BF), TOKEN],
        compiler_params=pltpu.CompilerParams(vmem_limit_bytes=6 * 2**20),
        cost_estimate=FREE,
    )(a, token)


def term_kernel(rows, nb, spots, kinds, n_recv, final, offs, *refs):
    refs = list(refs)
    parts = []
    for kind in kinds:
        ha, hb, d = refs.pop(0), refs.pop(0), [refs.pop(0) for _ in range(nb)]
        parts.append((ha, hb, d, kind, refs.pop(0)))
    recv = [refs.pop(0) for _ in range(n_recv)]
    out, token = refs[-2:]
    token[...] = jnp.zeros_like(token)
    tile = next(t for t in (160, 128, 112, 96, 80, 64, 48, 32, 16) if rows % t == 0)
    toks = (offs[0] * HALF, (1 - offs[0]) * HALF)
    for j in range(nb):
        cols = pl.ds(j * BLK, BLK)

        @pl.loop(0, rows // tile)
        def _(i):
            at = pl.multiple_of(i * tile, 16)
            here = pl.ds(at, tile)
            num = den = None
            for (ha, hb, d, kind, w), (h_spot, a_col, w_row_spot, w_col_spot) in zip(parts, spots):
                row = pl.multiple_of(offs[h_spot] + at, 16)
                w_row = pl.multiple_of(offs[w_row_spot] + at, 16)
                w_col = pl.multiple_of(offs[w_col_spot + j], BLK)
                weight = jnp.full((tile, BLK), fisher_floor, F32)
                for h, h_col, tok in zip((ha, hb), (a_col, 0), toks):
                    for e in range(2):
                        there = pl.ds(pl.multiple_of(tok + e * LEN, LEN), LEN)
                        grad = jnp.dot(
                            h[pl.ds(row, tile), h_col + e * LEN : h_col + (e + 1) * LEN],
                            d[j][there, :] if kind is None else d[j][kind, there, :],
                            preferred_element_type=F32,
                        )
                        weight = weight + grad * grad
                term = weight * w[pl.ds(w_row, tile), pl.ds(w_col, BLK)].astype(F32)
                num = term if num is None else num + term
                den = weight if den is None else den + weight
            for ref in recv:
                num = num + ref[0, here, cols].astype(F32)
                den = den + ref[1, here, cols].astype(F32)
            if final:
                out[here, cols] = (num / den).astype(BF)
            else:
                out[0, here, cols] = num.astype(BF)
                out[1, here, cols] = den.astype(BF)


def terms(offs, sources, rows, recv, final, before):
    nb = len(sources[0][2])
    wide = nb * BLK
    operands = [offs]
    for ha, hb, d, kind, w, spots in sources:
        operands += [ha, hb, *d, w]
    operands += [*recv, *before]
    return pl.pallas_call(
        functools.partial(term_kernel, rows, nb, [s[5] for s in sources], [s[3] for s in sources], len(recv), final),
        in_specs=[SMEM] + [VMEM] * (len(operands) - 1),
        out_specs=[VMEM, VMEM],
        out_shape=[jax.ShapeDtypeStruct((rows, wide) if final else (2, rows, wide), BF), TOKEN],
        compiler_params=pltpu.CompilerParams(vmem_limit_bytes=6 * 2**20),
        cost_estimate=FREE,
    )(*operands)


def merge_kernel(a, b, before, out, token):
    token[...] = jnp.zeros_like(token)
    num = a[0].astype(F32) + b[0].astype(F32)
    den = a[1].astype(F32) + b[1].astype(F32)
    out[...] = (num / den).astype(BF)


def merge(a, b, token):
    return pl.pallas_call(
        merge_kernel,
        in_specs=[VMEM] * 3,
        out_specs=[VMEM, VMEM],
        out_shape=[jax.ShapeDtypeStruct(a.shape[1:], BF), TOKEN],
        compiler_params=pltpu.CompilerParams(vmem_limit_bytes=6 * 2**20),
        cost_estimate=FREE,
    )(a, b, token)


def place_kernel(plan, n_parts, offs, *refs):
    parts, out, sem = refs[:n_parts], refs[-2], refs[-1]
    copies = []
    for part, lead, rows, row_at, col_at, nb in plan:
        src = parts[part] if lead is None else parts[part].at[lead]
        row = pl.multiple_of(offs[row_at], 16)
        for j in range(nb):
            col = pl.multiple_of(offs[col_at + j], BLK)
            copy = pltpu.make_async_copy(
                src.at[:, pl.ds(j * BLK, BLK)], out.at[pl.ds(row, rows), pl.ds(col, BLK)], sem.at[len(copies)]
            )
            copy.start()
            copies.append(copy)
    for copy in copies:
        copy.wait()


def place(shape, offs, parts, plan, before):
    return pl.pallas_call(
        functools.partial(place_kernel, plan, len(parts)),
        in_specs=[SMEM] + [VMEM] * (len(parts) + len(before)),
        out_specs=HBM,
        out_shape=jax.ShapeDtypeStruct(shape, BF),
        scratch_shapes=[pltpu.SemaphoreType.DMA((sum(p[-1] for p in plan),))],
        compiler_params=pltpu.CompilerParams(vmem_limit_bytes=2**20),
        cost_estimate=FREE,
    )(offs, *parts, *before)


def in_hbm(x):
    return pltpu.with_memory_space_constraint(x, pltpu.HBM)


def ints(*values):
    return jnp.stack([jnp.asarray(v, jnp.int32) for v in values])


def body(inputs, gate_weight, up_weight, cotangent, down_weight):
    task, core, col = lax.axis_index("task"), lax.axis_index("row"), lax.axis_index("col")
    y, h = task // 2, task % 2
    z_lo, x = col // 4, col % 4
    ring = 1 - 2 * core
    width, wide = down_weight.shape[1:]
    half, quarter, part = width // 2, width // 4, width // 8
    table = [core, (1 - h) * half, (1 - z_lo) * (wide // 2)]
    block = [(x - n) % 4 * BLK for n in range(4)]
    NEAR = len(table)
    table += [z_lo * (wide // 2) + b for b in block]
    FAR = len(table)
    table += [(1 - z_lo) * (wide // 2) + b for b in block]
    ALONE = len(table)
    table += block
    RING_ROW = len(table)
    table += [(y - k * ring) % 4 * quarter for k in range(4)]
    PART = len(table)
    table += [(y - k * ring) % 4 * part for k in range(4)]
    HERE = len(table)
    table += [h * half + (y - k * ring) % 4 * part for k in range(4)]
    BACK = len(table)
    table += [(y - k * ring) % 4 * quarter for k in range(4)]
    BACK_HERE = len(table)
    table += [h * half + (y - k * ring) % 4 * part for k in range(4)]
    BACK_AWAY = len(table)
    table += [(1 - h) * half + (y - k * ring) % 4 * part for k in range(4)]
    offs = ints(*table)

    mine = cotangent[0]
    near = [mine] + [move(mine, x_shift(n), "col") for n in (1, 2, 3)]
    far_mine = [move(mine, ZLO_SWAP, "col"), move(mine, Z_MIRROR, ("task", "col"))]
    w = down_weight[0]
    own, send, token = project(offs, inputs[0], gate_weight[0], up_weight[0])
    send, token = hold(send, [token, *far_mine, near[1], near[3], near[2]])
    ha, away, far_pair, token = make_hidden(offs, own, move(send, CORE_SWAP, "row"), w, far_mine, [token])
    hb = move(ha, CORE_SWAP, "row")
    far = [far_pair] + [move(far_pair, x_shift(n), "col") for n in (1, 2, 3)]
    za = move(away, Z_SWAP)

    def ring_terms(p, k, recv, *before):
        at = RING_ROW + k
        d = near[2 * p : 2 * p + 2]
        return terms(offs, [(ha, hb, d, None, w, (at, 0, at, NEAR + 2 * p))], quarter, recv, False, before)

    def far_terms(k, recv, final, *before):
        return terms(
            offs,
            [
                (ha, hb, far, 0, w, (HERE + k, 0, HERE + k, FAR)),
                (za, zb, far, 1, za, (PART + k, wide // 2, PART + k, ALONE)),
            ],
            part, recv, final, before,
        )

    def onward(piece):
        return move(piece, RING, ("task", "row"))

    got = [(), ()]
    for k in (1, 2, 3):
        for p in range(2):
            extra = {(2, 1): [far[1], far[3]], (3, 1): far[2:3]}.get((k, p), [])
            piece, token = ring_terms(p, k, got[p], token, *extra)
            got[p] = (move(piece, RING, ("task", "row")),)
    zb, token = cut(za, HALF, token)
    zb = move(zb, CORE_SWAP, "row")
    a_sum, a_got, a_all = [None, None], [None, None], [None, None]
    a_sum[0], token = ring_terms(0, 0, got[0], token)
    a_got[0] = move(a_sum[0], Z_SWAP)
    b_got, early = (), []
    for k in (1, 2, 3):
        piece, token = far_terms(k, b_got, False, token)
        b_got = (onward(piece),)
        if k == 1:
            a_sum[1], token = ring_terms(1, 0, got[1], token)
            a_got[1] = move(a_sum[1], Z_SWAP)
        if k == 2:
            out, token = merge(a_sum[0], a_got[0], token)
            a_all[0] = [out, onward(out)]
            early = [a_all[0][1]]
        if k == 3:
            a_all[0].append(onward(a_all[0][1]))
            out, token = merge(a_sum[1], a_got[1], token)
            a_all[1] = [out, onward(out)]
    b_out, token = far_terms(0, b_got, True, token)
    b_near = [b_out, onward(b_out)]
    b_far = [move(piece, Z_SWAP) for piece in b_near]
    b_near.append(onward(b_near[1]))
    a_all[1].append(onward(a_all[1][1]))
    b_near[2], _ = hold(b_near[2], [b_far[0]])
    b_near.append(onward(b_near[2]))
    b_far += [move(piece, Z_SWAP) for piece in b_near[2:]]
    for p in range(2):
        a_all[p][2], _ = hold(a_all[p][2], [b_far[1 + p]])
        a_all[p].append(onward(a_all[p][2]))

    plan = []
    for k in range(4):
        plan += [(4 * p + k, None, quarter, BACK + k, NEAR + 2 * p, 2) for p in range(2)]
        plan += [(8 + k, None, part, BACK_HERE + k, FAR, 4), (12 + k, None, part, BACK_AWAY + k, FAR, 4)]
    return place((width, wide), offs, [*a_all[0], *a_all[1], *b_near, *b_far], plan, [token])


def solution(mesh):
    placed = (
        P("task", None, "row"),
        P("task", "row", "col"),
        P("task", "row", "col"),
        P("task", None, ("row", "col")),
        P("task", "col", "row"),
    )
    return jax.shard_map(
        body, mesh=mesh, in_specs=placed, out_specs=P("col", "row"), check_vma=False
    )
```
